256 devices in a mesh: seq: 64 (over z_hi, x, y, core), chan: 4 (over z_lo).
Axes of the slice: x: 4, y: 4, z: 8 (z_hi: 2, z_lo: 4; z = z_hi * 4 + z_lo), core: 2. Of those that a mesh axis runs over, the one named last changes fastest.
Arguments:
- query_stream: bfloat16 [16384, 4096], P('seq', 'chan'), may hold values from -6 to 6
- key_stream: bfloat16 [16384, 4096], P('seq', 'chan'), may hold values from -6 to 6
- value_stream: bfloat16 [16384, 4096], P('seq', 'chan'), may hold values from -6 to 6
- short_filter: float32 [3, 3, 4096], P(None, None, 'chan'), may hold values from -3 to 3
- decay_rate: float32 [4096, 16], P('chan'), may hold values from 1.2207031e-05 to 0.034, as said below
- residues: float32 [4096, 16], P('chan'), may hold values from -0.3 to 0.3
- skip_bias: float32 [4096], P('chan'), may hold values from -4 to 4
- out_weight: bfloat16 [4096, 4096], P('chan'), may hold values from -0.09375 to 0.09375
Outputs:
- mixed: bfloat16 [16384, 4096], P(('seq', 'chan'))
The draws below stay inside these ranges and needn't reach their ends.
Inputs may be any that keep to these rules, and one draw needn't show every extreme that they name: `decay_rate`: each mode's rate is positive; some modes decay within a few tens of positions, others keep a large share of their weight over the whole sequence.
All inputs are finite; a program needn't handle non-finite values.
Results may differ from the reference program's by a relative error of at most 0.015.
Values may be sent and summed in bfloat16 or wider, within the bound.
No kernel may reach another device: no remote copies, remote signals or barrier semaphores. Data moves between devices by JAX's collectives and lax.ppermute only.
A program may use at most 256 MiB of HBM per device.

```python
import math
import jax
import jax.numpy as jnp
from jax import lax

D = 4096
C = 4096
MODES = 16
SHORT = 3
TOKENS = 16384


def mode_rates(key, slow_share, slow_low, slow_high):
    pick_key, slow_key, fast_key = jax.random.split(key, 3)
    slow_pick = jax.random.uniform(pick_key, (C, MODES)) < slow_share
    slow_rate = jnp.exp(jax.random.uniform(slow_key, (C, MODES), minval=jnp.log(slow_low), maxval=jnp.log(slow_high)))
    fast_rate = jnp.exp(jax.random.uniform(fast_key, (C, MODES), minval=jnp.log(1.0 / 60.0), maxval=jnp.log(1.0 / 30.0)))
    return jnp.where(slow_pick, slow_rate, fast_rate).astype(jnp.float32)


def draw_decay_rate(key, part):
    shared = mode_rates(key, 0.5, 0.2 / TOKENS, 2.0 / TOKENS)
    return shared


def draw_residues(key, part):
    shared = mode_rates(key, 0.5, 0.2 / TOKENS, 2.0 / TOKENS)
    key = jax.random.fold_in(key, 7)
    spread = jnp.sqrt(2.0 * shared / MODES)
    sample = jax.random.truncated_normal(key, -4.0, 4.0, (C, MODES))
    return jnp.clip(sample * spread, -0.3, 0.3).astype(jnp.float32)


def block_levels(key, shape, shards, low, largest):
    factor_of = 1.0
    for dim, parts in shards:
        heights = jax.random.uniform(jax.random.fold_in(jax.random.fold_in(key, 6), dim), (parts,), jnp.float32, low / len(shards), largest / len(shards))
        factor_of = factor_of * jnp.repeat(jnp.exp(heights), shape[dim] // parts).reshape((-1,) + (1,) * (len(shape) - 1 - dim))
    return factor_of


def centred(key, extent, scale, reach, cuts=(), kind=jnp.bfloat16):
    values = jax.random.normal(key, extent, jnp.float32) * scale
    if len(cuts) > 0:
        values = block_levels(key, extent, cuts, -0.22, 0.18) * values
    return jnp.clip(values, min=-reach, max=reach).astype(kind)


def setup_inputs(seed: int = 0) -> dict:
    key_of = jax.random.split(jax.random.key(seed), 9)
    return {
        "query_stream": centred(key_of[0], (TOKENS, C), 1.0, 6.0, ((0, 64), (1, 4))),
        "key_stream": centred(key_of[1], (TOKENS, C), 1.0, 6.0, ((0, 64), (1, 4))),
        "value_stream": centred(key_of[2], (TOKENS, C), 1.0, 6.0, ((0, 64), (1, 4))),
        "short_filter": centred(key_of[3], (3, SHORT, C), 0.6, 3.0, ((2, 4),), jnp.float32),
        "decay_rate": draw_decay_rate(jax.random.fold_in(key_of[8], 71), 0),
        "residues": draw_residues(jax.random.fold_in(key_of[8], 71), 0),
        "skip_bias": centred(key_of[6], (C,), 1.0, 4.0, ((0, 4),), jnp.float32),
        "out_weight": centred(key_of[7], (C, D), C ** -0.5, 0.09375, ((0, 4),)),
    }


def short_causal(stream, taps):
    values = stream.astype(jnp.float32)
    result = taps[0] * values
    for offset in range(1, SHORT):
        delayed = jnp.concatenate([jnp.zeros((offset, values.shape[1]), jnp.float32), values[:TOKENS - offset]], axis=0)
        result = result + taps[offset] * delayed
    return result


def long_block(operands):
    gated_block, rate_block, residue_block = operands
    moments = jnp.arange(TOKENS, dtype=jnp.float32)[:, None]
    kernel = jnp.zeros(gated_block.shape, jnp.float32)
    for mode_index in range(MODES):
        kernel = kernel + residue_block[:, mode_index] * jnp.exp(-rate_block[:, mode_index] * moments)
    signal = gated_block.astype(jnp.float32)
    product = jnp.fft.rfft(signal, n=2 * TOKENS, axis=0) * jnp.fft.rfft(kernel, n=2 * TOKENS, axis=0)
    return jnp.fft.irfft(product, n=2 * TOKENS, axis=0)[:TOKENS]


def reference(query_stream, key_stream, value_stream, short_filter, decay_rate, residues, skip_bias, out_weight):
    short_query = short_causal(query_stream, short_filter[0])
    short_key = short_causal(key_stream, short_filter[1])
    short_value = short_causal(value_stream, short_filter[2])
    gated = (short_key * short_value).astype(jnp.bfloat16)
    block_width = math.gcd(C, 128)
    blocks = C // block_width
    pieces = (gated.reshape(TOKENS, blocks, block_width).transpose(1, 0, 2),
              decay_rate.reshape(blocks, block_width, MODES),
              residues.reshape(blocks, block_width, MODES))
    long_term = lax.map(long_block, pieces).transpose(1, 0, 2).reshape(TOKENS, C)
    mixed_in = ((long_term + skip_bias * gated.astype(jnp.float32)) * short_query).astype(jnp.bfloat16)
    return jnp.dot(mixed_in, out_weight, preferred_element_type=jnp.float32).astype(jnp.bfloat16)
```

```python
import functools

import jax
import jax.numpy as jnp
from jax import lax
from jax.experimental import pallas as pl
from jax.experimental.pallas import tpu as pltpu
from jax.sharding import PartitionSpec as P

MODES = 16
SHORT = 3
F32 = jnp.float32
BF16 = jnp.bfloat16
LANES = 128
SUB = 8
PAD = 8
VMEM_LIMIT = 40 * 1024 * 1024


def short_taps(ext, taps_ref, stream, lanes, first, count):
    return (
        taps_ref[stream, 0:1, lanes] * ext[pl.ds(PAD + first, count), :]
        + taps_ref[stream, 1:2, lanes] * ext[pl.ds(PAD + first - 1, count), :]
        + taps_ref[stream, 2:3, lanes] * ext[pl.ds(PAD + first - 2, count), :]
    )


def fill_ext(ext, border_ref, stream_ref, stream, lanes, rows):
    ext[0:PAD, :] = jnp.zeros((PAD, LANES), F32)
    ext[PAD - 2 : PAD, :] = border_ref[stream, :, lanes].astype(F32)
    ext[PAD : PAD + rows, :] = stream_ref[:, lanes].astype(F32)


def state_kernel(border_ref, key_ref, value_ref, taps_ref, rate_ref, state_ref, gated_ref, ext_key, ext_value):
    rows = key_ref.shape[0]
    pitch = rows + PAD
    for group in range(SUB):
        lanes = slice(group * LANES, (group + 1) * LANES)
        fill_ext(ext_key, border_ref, key_ref, 1, lanes, rows)
        fill_ext(ext_value, border_ref, value_ref, 2, lanes, rows)
        gated = short_taps(ext_key, taps_ref, 1, lanes, 0, rows) * short_taps(ext_value, taps_ref, 2, lanes, 0, rows)
        gated_ref[group * pitch : group * pitch + rows, :] = gated.astype(BF16).astype(F32)
        gated_ref[group * pitch + rows : (group + 1) * pitch, :] = jnp.zeros((PAD, LANES), F32)
    decay = [jnp.exp(-rate_ref[m]) for m in range(MODES)]

    def step(t, carry):
        now = gated_ref[pl.ds(t, SUB, stride=pitch), :]
        return tuple(decay[m] * carry[m] + now for m in range(MODES))

    final = lax.fori_loop(0, rows, step, tuple(jnp.zeros((SUB, LANES), F32) for _ in range(MODES)), unroll=8)
    for m in range(MODES):
        state_ref[m] = final[m]


def local_kernel(border_ref, query_ref, gated_ref, taps_ref, rate_ref, residue_ref, skip_ref, local_ref, query_out_ref, ext, conv):
    rows = query_ref.shape[0]
    pitch = rows + PAD
    decay = [jnp.exp(-rate_ref[m]) for m in range(MODES)]

    def step(t, carry):
        now = gated_ref[pl.ds(t, SUB, stride=pitch), :]
        fresh = tuple(decay[m] * carry[m] + now for m in range(MODES))
        terms = [residue_ref[m] * fresh[m] for m in range(MODES)]
        while len(terms) > 1:
            terms = [terms[i] + terms[i + 1] for i in range(0, len(terms), 2)]
        conv[pl.ds(t, SUB, stride=pitch), :] = terms[0]
        return fresh

    lax.fori_loop(0, rows, step, tuple(jnp.zeros((SUB, LANES), F32) for _ in range(MODES)), unroll=4)
    for group in range(SUB):
        lanes = slice(group * LANES, (group + 1) * LANES)
        spot = slice(group * pitch, group * pitch + rows)
        local_ref[:, lanes] = conv[spot, :] + skip_ref[0:1, lanes] * gated_ref[spot, :]
        fill_ext(ext, border_ref, query_ref, 0, lanes, rows)
        query_out_ref[:, lanes] = short_taps(ext, taps_ref, 0, lanes, 0, rows)


def mix_kernel(local_ref, query_ref, start_ref, rate_ref, residue_ref, mixed_ref):
    rows = local_ref.shape[0]
    phase = lax.broadcasted_iota(jnp.int32, (SUB, LANES), 0).astype(F32) + 1.0
    for group in range(SUB):
        lanes = slice(group * LANES, (group + 1) * LANES)
        line = slice(group, group + 1)
        carry, decay = [], []
        for m in range(MODES):
            rate = rate_ref[m, line, :]
            carry.append(jnp.exp(-rate * phase) * (residue_ref[m, line, :] * start_ref[m, line, :]))
            decay.append(jnp.broadcast_to(jnp.exp(-rate * float(SUB)), (SUB, LANES)))
        for tile in range(0, rows, 2 * SUB):
            parts = []
            for half in range(2):
                spot = slice(tile + half * SUB, tile + (half + 1) * SUB)
                terms = list(carry)
                while len(terms) > 1:
                    terms = [terms[i] + terms[i + 1] for i in range(0, len(terms), 2)]
                parts.append((local_ref[spot, lanes] + terms[0]) * query_ref[spot, lanes])
                carry = [carry[m] * decay[m] for m in range(MODES)]
            mixed_ref[tile : tile + 2 * SUB, lanes] = jnp.concatenate(parts, axis=0).astype(BF16)


def whole(count):
    return [pl.BlockSpec(memory_space=pltpu.VMEM)] * count


def levels_of(count):
    levels, left = [], count
    if left % 2 == 0:
        levels.append(2)
        left //= 2
    while left % 4 == 0:
        levels.append(4)
        left //= 4
    if left > 1:
        levels.append(left)
    return levels


def scan_states(state, rate, rows):
    count = lax.axis_size("seq")
    place = lax.axis_index("seq")
    total, start, width = state, jnp.zeros_like(state), 1
    levels = levels_of(count)
    for position, radix in enumerate(levels):
        me = (place // width) % radix
        low = (place % width).astype(F32)
        others = [
            lax.ppermute(total.astype(BF16), "seq", [(j, j ^ (width * s)) for j in range(count)])
            for s in range(1, radix)
        ]
        for s in range(1, radix):
            other = me ^ s
            gap = jnp.maximum(me - 1 - other, 0).astype(F32)
            weight = jnp.where(other < me, jnp.exp(-rate * (rows * (width * gap + low))), 0.0)
            start = start + weight * others[s - 1].astype(F32)
        if position < len(levels) - 1:
            fresh = total * jnp.exp(-rate * (rows * width * (radix - 1 - me).astype(F32)))
            for s in range(1, radix):
                other = me ^ s
                fresh = fresh + others[s - 1].astype(F32) * jnp.exp(
                    -rate * (rows * width * (radix - 1 - other).astype(F32))
                )
            total = fresh
        width *= radix
    return start


def on_device(query_stream, key_stream, value_stream, short_filter, decay_rate, residues, skip_bias, out_weight):
    rows, channels = query_stream.shape
    assert channels == SUB * LANES
    pitch = rows + PAD
    count = lax.axis_size("seq")
    tails = jnp.stack([query_stream[rows - 2 :], key_stream[rows - 2 :], value_stream[rows - 2 :]])
    border = lax.ppermute(tails, "seq", [(j, j + 1) for j in range(count - 1)])
    rate = decay_rate.T.reshape(MODES, SUB, LANES)
    residue = residues.T.reshape(MODES, SUB, LANES)
    params = pltpu.CompilerParams(vmem_limit_bytes=VMEM_LIMIT)
    state, gated = pl.pallas_call(
        state_kernel,
        out_shape=(
            jax.ShapeDtypeStruct((MODES, SUB, LANES), F32),
            jax.ShapeDtypeStruct((SUB * pitch, LANES), F32),
        ),
        in_specs=whole(5),
        out_specs=tuple(whole(2)),
        scratch_shapes=[pltpu.VMEM((pitch, LANES), F32)] * 2,
        compiler_params=params,
    )(border, key_stream, value_stream, short_filter, rate)
    local, query = pl.pallas_call(
        local_kernel,
        out_shape=(jax.ShapeDtypeStruct((rows, channels), F32),) * 2,
        in_specs=whole(7),
        out_specs=tuple(whole(2)),
        scratch_shapes=[pltpu.VMEM((pitch, LANES), F32), pltpu.VMEM((SUB * pitch, LANES), F32)],
        compiler_params=params,
    )(border, query_stream, gated, short_filter, rate, residue, skip_bias[None])
    start = scan_states(state, rate, float(rows))
    mixed_in = pl.pallas_call(
        mix_kernel,
        out_shape=jax.ShapeDtypeStruct((rows, channels), BF16),
        in_specs=whole(5),
        out_specs=whole(1)[0],
        compiler_params=params,
    )(local, query, start, rate, residue)
    parts = lax.axis_size("chan")
    mine = lax.axis_index("chan")
    piece = rows // parts
    partial = jnp.dot(mixed_in, out_weight, preferred_element_type=F32)
    blocks = partial.astype(BF16).reshape(parts, piece, -1)
    summed = lax.dynamic_slice_in_dim(partial, mine * piece, piece, 0)
    for step in (2, 3, 1):
        block = lax.dynamic_index_in_dim(blocks, mine ^ step, 0, False)
        summed = summed + lax.ppermute(block, "chan", [(j, j ^ step) for j in range(parts)]).astype(F32)
    return summed.astype(BF16)


def solution(mesh):
    return jax.shard_map(
        on_device,
        mesh=mesh,
        in_specs=(
            P("seq", "chan"),
            P("seq", "chan"),
            P("seq", "chan"),
            P(None, None, "chan"),
            P("chan", None),
            P("chan", None),
            P("chan"),
            P("chan", None),
        ),
        out_specs=P(("seq", "chan"), None),
        check_vma=False,
    )
```

```python
import jax
import jax.numpy as jnp
from jax import lax
from jax.experimental import pallas as pl
from jax.experimental.pallas import tpu as pltpu
from jax.sharding import PartitionSpec as P

MODES = 16
SHORT = 3
F32 = jnp.float32
BF16 = jnp.bfloat16
LANES = 128
SUB = 8
PAD = 8
STATE_ROWS = MODES * SUB
HEADS = 4
TAILS = 6
PAYLOAD = STATE_ROWS + SUB * (HEADS + TAILS)
COLUMN_TILE = 512
CUTS = 4
WEIGHT_CUTS = 8
VMEM_LIMIT = 28 * 1024 * 1024
HBM = pl.BlockSpec(memory_space=pltpu.HBM)
VMEM = pl.BlockSpec(memory_space=pltpu.VMEM)
SMEM = pl.BlockSpec(memory_space=pltpu.SMEM)


def summed(terms):
    terms = list(terms)
    while len(terms) > 1:
        terms = [terms[i] + terms[i + 1] for i in range(0, len(terms), 2)]
    return terms[0]


def short_taps(ext, taps_ref, stream, lanes, count):
    return (
        taps_ref[stream, 0:1, lanes] * ext[PAD : PAD + count, :]
        + taps_ref[stream, 1:2, lanes] * ext[PAD - 1 : PAD - 1 + count, :]
        + taps_ref[stream, 2:3, lanes] * ext[PAD - 2 : PAD - 2 + count, :]
    )


def to_rows(source, target):
    for group in range(SUB):
        target[pl.ds(group, MODES, stride=SUB), :] = source[:, group * LANES : (group + 1) * LANES]


def copies(pairs, sems):
    made = [pltpu.make_async_copy(a, b, sems.at[i]) for i, (a, b) in enumerate(pairs)]
    for one in made:
        one.start()
    return made


def state_kernel(
    query_hbm, key_hbm, value_hbm, taps_hbm, rate_hbm,
    payload_ref, sent_ref, rate_ref, gated_ref, taps_ref,
    key_buf, value_buf, query_buf, taps_buf, rate_buf, ext_key, ext_value, sems,
):
    rows, channels = key_buf.shape
    pitch = rows + PAD
    width = channels // CUTS
    made = copies(
        [(rate_hbm, rate_buf), (taps_hbm, taps_buf)]
        + [
            (hbm.at[:, pl.ds(part * width, width)], buf.at[:, pl.ds(part * width, width)])
            for part in range(CUTS)
            for hbm, buf in ((key_hbm, key_buf), (value_hbm, value_buf))
        ]
        + [(query_hbm.at[pl.ds(rows - 16, 16), :], query_buf)],
        sems,
    )
    ext_key[0:PAD, :] = jnp.zeros((PAD, LANES), F32)
    ext_value[0:PAD, :] = jnp.zeros((PAD, LANES), F32)
    made[0].wait()
    to_rows(rate_buf, rate_ref)
    made[1].wait()
    for group in range(SUB):
        if group % (SUB // CUTS) == 0:
            part = group // (SUB // CUTS)
            made[2 + 2 * part].wait()
            made[3 + 2 * part].wait()
        lanes = slice(group * LANES, (group + 1) * LANES)
        ext_key[PAD : PAD + rows, :] = key_buf[:, lanes].astype(F32)
        ext_value[PAD : PAD + rows, :] = value_buf[:, lanes].astype(F32)
        gated = short_taps(ext_key, taps_buf, 1, lanes, rows) * short_taps(ext_value, taps_buf, 2, lanes, rows)
        base = group * pitch
        gated_ref[base : base + rows, :] = gated.astype(BF16).astype(F32)
        gated_ref[base : base + 2, :] = jnp.zeros((2, LANES), F32)
        gated_ref[base + rows : base + pitch, :] = jnp.zeros((PAD, LANES), F32)
        for place, (ext, row) in enumerate(
            ((ext_key, 0), (ext_key, 1), (ext_value, 0), (ext_value, 1))
        ):
            at = STATE_ROWS + place * SUB + group
            payload_ref[at : at + 1, :] = ext[PAD + row : PAD + row + 1, :]
        for place, (ext, row) in enumerate(
            ((ext_key, rows - 2), (ext_key, rows - 1), (ext_value, rows - 2), (ext_value, rows - 1))
        ):
            at = STATE_ROWS + (HEADS + 2 + place) * SUB + group
            payload_ref[at : at + 1, :] = ext[PAD + row : PAD + row + 1, :]
    decay = [jnp.exp(-rate_ref[m * SUB : (m + 1) * SUB, :]) for m in range(MODES)]

    def step(t, carry):
        now = gated_ref[pl.ds(t, SUB, stride=pitch), :]
        return tuple(decay[m] * carry[m] + now for m in range(MODES))

    final = lax.fori_loop(0, rows, step, tuple(jnp.zeros((SUB, LANES), F32) for _ in range(MODES)), unroll=8)
    for m in range(MODES):
        payload_ref[m * SUB : (m + 1) * SUB, :] = final[m]
    made[2 + 2 * CUTS].wait()
    last = query_buf[...].astype(F32)
    for place, row in enumerate((14, 15)):
        for group in range(SUB):
            at = STATE_ROWS + (HEADS + place) * SUB + group
            payload_ref[at : at + 1, :] = last[row : row + 1, group * LANES : (group + 1) * LANES]
    sent_ref[...] = payload_ref[...].astype(BF16)
    for stream in range(3):
        for tap in range(SHORT):
            for group in range(SUB):
                at = (stream * SHORT + tap) * SUB + group
                taps_ref[at : at + 1, :] = taps_buf[stream, tap : tap + 1, group * LANES : (group + 1) * LANES]


def local_kernel(
    query_hbm, residue_hbm, skip_hbm, weight_hbm, gated_ref, rate_ref, taps_ref,
    local_ref, query_ref, residue_ref, weight_ref,
    query_buf, residue_buf, skip_buf, ext, conv, sems,
):
    rows = query_buf.shape[0]
    pitch = rows + PAD
    depth = weight_ref.shape[0] // WEIGHT_CUTS
    made = copies(
        [(residue_hbm, residue_buf), (query_hbm, query_buf), (skip_hbm, skip_buf)]
        + [
            (weight_hbm.at[pl.ds(i * depth, depth), :], weight_ref.at[pl.ds(i * depth, depth), :])
            for i in range(WEIGHT_CUTS)
        ],
        sems,
    )
    decay = [jnp.exp(-rate_ref[m * SUB : (m + 1) * SUB, :]) for m in range(MODES)]
    made[0].wait()
    to_rows(residue_buf, residue_ref)

    def step(t, carry):
        now = gated_ref[pl.ds(t, SUB, stride=pitch), :]
        fresh = tuple(decay[m] * carry[m] + now for m in range(MODES))
        conv[pl.ds(t, SUB, stride=pitch), :] = summed(
            residue_ref[m * SUB : (m + 1) * SUB, :] * fresh[m] for m in range(MODES)
        )
        return fresh

    lax.fori_loop(0, rows, step, tuple(jnp.zeros((SUB, LANES), F32) for _ in range(MODES)), unroll=4)
    made[1].wait()
    made[2].wait()
    ext[0:PAD, :] = jnp.zeros((PAD, LANES), F32)
    for group in range(SUB):
        lanes = slice(group * LANES, (group + 1) * LANES)
        spot = slice(group * pitch, group * pitch + rows)
        local_ref[:, lanes] = conv[spot, :] + skip_buf[group : group + 1, :] * gated_ref[spot, :]
        ext[PAD : PAD + rows, :] = query_buf[:, lanes].astype(F32)
        tap = [taps_ref[p * SUB + group : p * SUB + group + 1, :] for p in range(SHORT)]
        query_ref[:, lanes] = (
            tap[0] * ext[PAD : PAD + rows, :]
            + tap[1] * ext[PAD - 1 : PAD - 1 + rows, :]
            + tap[2] * ext[PAD - 2 : PAD - 2 + rows, :]
        )
    for one in made[3:]:
        one.wait()


def mix_kernel(
    place_ref, local_ref, query_ref, after_ref, fix_ref, rate_ref, residue_ref, weight_ref,
    first_ref, second_ref,
    mixed, coef,
):
    half_rows, depth = mixed.shape
    piece = half_rows // 2
    columns = weight_ref.shape[1]
    base = place_ref[0]
    swap = place_ref[1]
    before = (base - 1).astype(F32)
    coef[...] = residue_ref[...] * after_ref[...] * jnp.exp(-rate_ref[...] * before)
    phase = lax.broadcasted_iota(jnp.int32, (SUB, LANES), 0)
    at_start = base == 0
    row_zero = jnp.logical_and(phase == 0, at_start)
    row_one = jnp.logical_and(phase == 1, at_start)
    zero = jnp.zeros((SUB, LANES), F32)
    for group in range(SUB):
        lanes = slice(group * LANES, (group + 1) * LANES)
        carry, decay = [], []
        for m in range(MODES):
            line = slice(m * SUB + group, m * SUB + group + 1)
            rate = rate_ref[line, :]
            carry.append(jnp.exp(-rate * phase.astype(F32)) * coef[line, :])
            decay.append(jnp.broadcast_to(jnp.exp(-rate * float(SUB)), (SUB, LANES)))

        def fix(i):
            return jnp.broadcast_to(fix_ref[i * SUB + group : i * SUB + group + 1, :], (SUB, LANES))

        for tile in range(0, half_rows, 2 * SUB):
            parts = []
            for inner in range(2):
                offset = tile + inner * SUB
                spot = pl.ds(pl.multiple_of(base + offset, SUB), SUB)
                carried = summed(carry)
                query = query_ref[spot, lanes]
                if offset == 0:
                    carried = jnp.where(row_zero, fix(0), carried) + jnp.where(row_one, fix(1), zero)
                    query = query + jnp.where(row_zero, fix(2), zero) + jnp.where(row_one, fix(3), zero)
                parts.append((local_ref[spot, lanes] + carried) * query)
                carry = [carry[m] * decay[m] for m in range(MODES)]
            block = tile // piece
            row = pl.multiple_of((block ^ swap) * piece + tile % piece, 2 * SUB)
            mixed[pl.ds(row, 2 * SUB), lanes] = jnp.concatenate(parts, axis=0).astype(BF16)
    for i in range(columns // COLUMN_TILE):
        where = slice(i * COLUMN_TILE, (i + 1) * COLUMN_TILE)
        product = jnp.dot(mixed[...], weight_ref[:, where], preferred_element_type=F32)
        first_ref[:, where] = product[:piece].astype(first_ref.dtype)
        second_ref[:, where] = product[piece:].astype(second_ref.dtype)


def scan_states(payload, sent, rate, taps, rows, place, count):
    tap = taps.reshape(3, SHORT, SUB, LANES)

    def head_gated(tail, head):
        def filtered(s, first, second, older, newer):
            return (
                tap[s][0] * first + tap[s][1] * newer + tap[s][2] * older,
                tap[s][0] * second + tap[s][1] * first + tap[s][2] * newer,
            )

        keys = filtered(1, head[0], head[1], tail[2], tail[3])
        values = filtered(2, head[2], head[3], tail[4], tail[5])
        return [(k * v).astype(BF16).astype(F32) for k, v in zip(keys, values, strict=True)]

    def decayed(steps):
        return jnp.exp(-rate * steps)

    def joined(pair):
        return decayed(1.0) * pair[0] + pair[1]

    mine = payload.reshape(-1, SUB, LANES)
    own_head = mine[MODES : MODES + HEADS]
    total, head, tail = mine[:MODES], own_head, mine[MODES + HEADS :]
    start = jnp.zeros_like(total)
    border = jnp.zeros_like(tail)
    bits = (count - 1).bit_length()
    for bit in range(bits):
        width = 1 << bit
        mask = width
        if bit >= 2 and bit % 2 == 0 and bit < bits:
            mask = width | (width >> 1)
        got = lax.ppermute(sent, "seq", [(j, j ^ mask) for j in range(count)])
        theirs = got.reshape(-1, SUB, LANES).astype(F32)
        upper = ((place >> bit) & 1) == 1
        low = place % width
        length = rows * width
        other_total, other_head, other_tail = theirs[:MODES], theirs[MODES : MODES + HEADS], theirs[MODES + HEADS :]
        low_total = jnp.where(upper, other_total, total)
        low_tail = jnp.where(upper, other_tail, tail)
        high_head = jnp.where(upper, head, other_head)
        entry = joined(head_gated(low_tail, high_head))
        gone = (rows * low).astype(F32)
        start = start + jnp.where(
            upper,
            decayed(gone) * other_total
            + jnp.where(low > 0, decayed(jnp.maximum(gone - 2.0, 0.0)) * entry, 0.0),
            0.0,
        )
        border = jnp.where(jnp.logical_and(upper, low == 0), other_tail, border)
        if bit < bits - 1:
            high_total = jnp.where(upper, total, other_total)
            total = decayed(float(length)) * low_total + high_total + decayed(float(length - 2)) * entry
            tail = jnp.where(upper, tail, other_tail)
        head = jnp.where(upper, other_head, head)
        if bit < bits - 1:
            sent = jnp.concatenate([total, head, tail]).reshape(-1, LANES).astype(BF16)
    first = joined(head_gated(jnp.zeros_like(border), head))
    gone = (rows * place).astype(F32)
    start = start + jnp.where(place > 0, decayed(jnp.maximum(gone - 2.0, 0.0)) * first, 0.0)
    return start, border, head_gated(border, own_head), tap


def on_device(query_stream, key_stream, value_stream, short_filter, decay_rate, residues, skip_bias, out_weight):
    rows, channels = query_stream.shape
    assert channels == SUB * LANES
    columns = out_weight.shape[1]
    pitch = rows + PAD
    count = lax.axis_size("seq")
    place = lax.axis_index("seq")
    parts = lax.axis_size("chan")
    mine = lax.axis_index("chan")
    assert parts == 4
    piece = rows // parts
    query_stream, key_stream, value_stream, short_filter, out_weight, rates, residues, skips = (
        pltpu.with_memory_space_constraint(array, pltpu.HBM)
        for array in (
            query_stream, key_stream, value_stream, short_filter, out_weight,
            decay_rate.T, residues.T, skip_bias.reshape(SUB, LANES),
        )
    )
    params = pltpu.CompilerParams(vmem_limit_bytes=VMEM_LIMIT)
    dma = pltpu.SemaphoreType.DMA
    payload, sent, rate, gated, taps = pl.pallas_call(
        state_kernel,
        out_shape=(
            jax.ShapeDtypeStruct((PAYLOAD, LANES), F32),
            jax.ShapeDtypeStruct((PAYLOAD, LANES), BF16),
            jax.ShapeDtypeStruct((STATE_ROWS, LANES), F32),
            jax.ShapeDtypeStruct((SUB * pitch, LANES), F32),
            jax.ShapeDtypeStruct((3 * SHORT * SUB, LANES), F32),
        ),
        in_specs=[HBM] * 5,
        out_specs=(VMEM,) * 5,
        scratch_shapes=[
            pltpu.VMEM((rows, channels), BF16),
            pltpu.VMEM((rows, channels), BF16),
            pltpu.VMEM((16, channels), BF16),
            pltpu.VMEM((3, SHORT, channels), F32),
            pltpu.VMEM((MODES, channels), F32),
            pltpu.VMEM((pitch, LANES), F32),
            pltpu.VMEM((pitch, LANES), F32),
            dma((3 + 2 * CUTS,)),
        ],
        compiler_params=params,
        cost_estimate=pl.CostEstimate(flops=20_000_000, bytes_accessed=3_000_000, transcendentals=0),
    )(query_stream, key_stream, value_stream, short_filter, rates)
    local, query, residue, weight = pl.pallas_call(
        local_kernel,
        out_shape=(
            jax.ShapeDtypeStruct((rows, channels), F32),
            jax.ShapeDtypeStruct((rows, channels), F32),
            jax.ShapeDtypeStruct((STATE_ROWS, LANES), F32),
            jax.ShapeDtypeStruct(out_weight.shape, BF16),
        ),
        in_specs=[HBM] * 4 + [VMEM] * 3,
        out_specs=(VMEM,) * 4,
        scratch_shapes=[
            pltpu.VMEM((rows, channels), BF16),
            pltpu.VMEM((MODES, channels), F32),
            pltpu.VMEM((SUB, LANES), F32),
            pltpu.VMEM((pitch, LANES), F32),
            pltpu.VMEM((SUB * pitch, LANES), F32),
            dma((3 + WEIGHT_CUTS,)),
        ],
        compiler_params=params,
        cost_estimate=pl.CostEstimate(flops=20_000_000, bytes_accessed=6_000_000, transcendentals=0),
    )(query_stream, residues, skips, out_weight, gated, rate, taps)
    rate_rows = rate.reshape(MODES, SUB, LANES)
    residue_rows = residue.reshape(MODES, SUB, LANES)
    start, border, gates, tap = scan_states(payload, sent, rate_rows, taps, rows, place, count)
    skip = skip_bias.reshape(SUB, LANES)
    after_zero = jnp.exp(-rate_rows) * start + gates[0]
    after_one = jnp.exp(-rate_rows) * after_zero + gates[1]
    fixes = jnp.concatenate(
        [
            jnp.sum(residue_rows * after_zero, axis=0) + skip * gates[0],
            skip * gates[1],
            tap[0][1] * border[1] + tap[0][2] * border[0],
            tap[0][2] * border[1],
        ]
    )

    def mix(half, swap, second_type):
        return pl.pallas_call(
            mix_kernel,
            out_shape=(
                jax.ShapeDtypeStruct((piece, columns), BF16),
                jax.ShapeDtypeStruct((piece, columns), second_type),
            ),
            in_specs=[SMEM] + [VMEM] * 7,
            out_specs=(VMEM,) * 2,
            scratch_shapes=[
                pltpu.VMEM((2 * piece, channels), BF16),
                pltpu.VMEM((STATE_ROWS, LANES), F32),
            ],
            compiler_params=params,
            cost_estimate=pl.CostEstimate(flops=1_000_000_000, bytes_accessed=10_000_000, transcendentals=0),
        )(
            jnp.stack([half * 2 * piece, swap]).astype(jnp.int32),
            local, query, after_one.reshape(STATE_ROWS, LANES), fixes, rate, residue, weight,
        )

    own_half, odd = mine // 2, mine % 2
    across_two, across_three = mix(1 - own_half, odd, BF16)
    beside, own = mix(own_half, 1 - odd, F32)

    def sent_by(block, step):
        return lax.ppermute(block, "chan", [(j, j ^ step) for j in range(parts)]).astype(F32)

    total = own + sent_by(across_two, 2) + sent_by(across_three, 3) + sent_by(beside, 1)
    return total.astype(BF16)


def solution(mesh):
    return jax.shard_map(
        on_device,
        mesh=mesh,
        in_specs=(
            P("seq", "chan"),
            P("seq", "chan"),
            P("seq", "chan"),
            P(None, None, "chan"),
            P("chan", None),
            P("chan", None),
            P("chan"),
            P("chan", None),
        ),
        out_specs=P(("seq", "chan"), None),
        check_vma=False,
    )
```

```python
import jax
import jax.numpy as jnp
from jax import lax
from jax.experimental import pallas as pl
from jax.experimental.pallas import tpu as pltpu
from jax.sharding import PartitionSpec as P

MODES = 16
SHORT = 3
F32 = jnp.float32
BF16 = jnp.bfloat16
LANES = 128
SUB = 8
PAD = 8
STATE_ROWS = MODES * SUB
HEADS = 4
TAILS = 6
PAYLOAD = STATE_ROWS + SUB * (HEADS + TAILS)
COLUMN_TILE = 512
RIGHT_TILES = 5
CUTS = 4
VMEM_LIMIT = 20 * 1024 * 1024
HBM = pl.BlockSpec(memory_space=pltpu.HBM)
VMEM = pl.BlockSpec(memory_space=pltpu.VMEM)
SMEM = pl.BlockSpec(memory_space=pltpu.SMEM)


def summed(terms):
    terms = list(terms)
    while len(terms) > 1:
        terms = [terms[i] + terms[i + 1] for i in range(0, len(terms), 2)]
    return terms[0]


def short_taps(ext, taps_ref, stream, lanes, count):
    return (
        taps_ref[stream, 0:1, lanes] * ext[PAD : PAD + count, :]
        + taps_ref[stream, 1:2, lanes] * ext[PAD - 1 : PAD - 1 + count, :]
        + taps_ref[stream, 2:3, lanes] * ext[PAD - 2 : PAD - 2 + count, :]
    )


def to_rows(source, target):
    for group in range(SUB):
        target[pl.ds(group, MODES, stride=SUB), :] = source[:, group * LANES : (group + 1) * LANES]


def copies(pairs, sems):
    made = [pltpu.make_async_copy(a, b, sems.at[i]) for i, (a, b) in enumerate(pairs)]
    for one in made:
        one.start()
    return made


def fetch_weight(weight_hbm, weight_buf, sems, first):
    tiles, _, width = weight_buf.shape
    made = [
        pltpu.make_async_copy(weight_hbm.at[:, pl.ds(first + i * width, width)], weight_buf.at[i], sems.at[i])
        for i in range(tiles)
    ]
    for one in made:
        one.start()
    return made


def state_kernel(
    query_hbm, key_hbm, value_hbm, taps_hbm, rate_hbm, residue_hbm, skip_hbm,
    payload_ref, sent_ref, rate_ref, gated_ref, taps_ref, residue_ref, skip_ref,
    key_buf, value_buf, query_buf, taps_buf, rate_buf, residue_buf, ext_key, ext_value, sems,
):
    rows, channels = key_buf.shape
    pitch = rows + PAD
    width = channels // CUTS
    made = copies(
        [(rate_hbm, rate_buf), (taps_hbm, taps_buf)]
        + [
            (hbm.at[:, pl.ds(part * width, width)], buf.at[:, pl.ds(part * width, width)])
            for part in range(CUTS)
            for hbm, buf in ((key_hbm, key_buf), (value_hbm, value_buf))
        ]
        + [(query_hbm.at[pl.ds(rows - 16, 16), :], query_buf), (residue_hbm, residue_buf), (skip_hbm, skip_ref)],
        sems,
    )
    ext_key[0:PAD, :] = jnp.zeros((PAD, LANES), F32)
    ext_value[0:PAD, :] = jnp.zeros((PAD, LANES), F32)
    made[0].wait()
    to_rows(rate_buf, rate_ref)
    made[1].wait()
    for group in range(SUB):
        if group % (SUB // CUTS) == 0:
            part = group // (SUB // CUTS)
            made[2 + 2 * part].wait()
            made[3 + 2 * part].wait()
        lanes = slice(group * LANES, (group + 1) * LANES)
        ext_key[PAD : PAD + rows, :] = key_buf[:, lanes].astype(F32)
        ext_value[PAD : PAD + rows, :] = value_buf[:, lanes].astype(F32)
        gated = short_taps(ext_key, taps_buf, 1, lanes, rows) * short_taps(ext_value, taps_buf, 2, lanes, rows)
        base = group * pitch
        gated_ref[base : base + rows, :] = gated.astype(BF16).astype(F32)
        gated_ref[base : base + 2, :] = jnp.zeros((2, LANES), F32)
        gated_ref[base + rows : base + pitch, :] = jnp.zeros((PAD, LANES), F32)
        for place, (ext, row) in enumerate(
            ((ext_key, 0), (ext_key, 1), (ext_value, 0), (ext_value, 1))
        ):
            at = STATE_ROWS + place * SUB + group
            payload_ref[at : at + 1, :] = ext[PAD + row : PAD + row + 1, :]
        for place, (ext, row) in enumerate(
            ((ext_key, rows - 2), (ext_key, rows - 1), (ext_value, rows - 2), (ext_value, rows - 1))
        ):
            at = STATE_ROWS + (HEADS + 2 + place) * SUB + group
            payload_ref[at : at + 1, :] = ext[PAD + row : PAD + row + 1, :]
    decay = [jnp.exp(-rate_ref[m * SUB : (m + 1) * SUB, :]) for m in range(MODES)]

    def step(t, carry):
        now = gated_ref[pl.ds(t, SUB, stride=pitch), :]
        return tuple(decay[m] * carry[m] + now for m in range(MODES))

    final = lax.fori_loop(0, rows, step, tuple(jnp.zeros((SUB, LANES), F32) for _ in range(MODES)), unroll=8)
    for m in range(MODES):
        payload_ref[m * SUB : (m + 1) * SUB, :] = final[m]
    for one in made[2 + 2 * CUTS :]:
        one.wait()
    to_rows(residue_buf, residue_ref)
    last = query_buf[...].astype(F32)
    for place, row in enumerate((14, 15)):
        for group in range(SUB):
            at = STATE_ROWS + (HEADS + place) * SUB + group
            payload_ref[at : at + 1, :] = last[row : row + 1, group * LANES : (group + 1) * LANES]
    sent_ref[...] = payload_ref[...].astype(BF16)
    for stream in range(3):
        for tap in range(SHORT):
            for group in range(SUB):
                at = (stream * SHORT + tap) * SUB + group
                taps_ref[at : at + 1, :] = taps_buf[stream, tap : tap + 1, group * LANES : (group + 1) * LANES]


def local_kernel(gated_ref, rate_ref, residue_ref, skip_ref, local_ref, conv):
    rows = local_ref.shape[0]
    pitch = rows + PAD
    decay = [jnp.exp(-rate_ref[m * SUB : (m + 1) * SUB, :]) for m in range(MODES)]

    def step(t, carry):
        now = gated_ref[pl.ds(t, SUB, stride=pitch), :]
        fresh = tuple(decay[m] * carry[m] + now for m in range(MODES))
        conv[pl.ds(t, SUB, stride=pitch), :] = summed(
            residue_ref[m * SUB : (m + 1) * SUB, :] * fresh[m] for m in range(MODES)
        )
        return fresh

    lax.fori_loop(0, rows, step, tuple(jnp.zeros((SUB, LANES), F32) for _ in range(MODES)), unroll=8)
    for group in range(SUB):
        lanes = slice(group * LANES, (group + 1) * LANES)
        spot = slice(group * pitch, group * pitch + rows)
        local_ref[:, lanes] = conv[spot, :] + skip_ref[group : group + 1, :] * gated_ref[spot, :]


def query_kernel(query_hbm, taps_ref, query_ref, query_buf, ext, sems):
    rows = query_ref.shape[0]
    made = copies([(query_hbm, query_buf)], sems)
    ext[0:PAD, :] = jnp.zeros((PAD, LANES), F32)
    made[0].wait()
    for group in range(SUB):
        lanes = slice(group * LANES, (group + 1) * LANES)
        ext[PAD : PAD + rows, :] = query_buf[:, lanes].astype(F32)
        tap = [taps_ref[p * SUB + group : p * SUB + group + 1, :] for p in range(SHORT)]
        query_ref[:, lanes] = (
            tap[0] * ext[PAD : PAD + rows, :]
            + tap[1] * ext[PAD - 1 : PAD - 1 + rows, :]
            + tap[2] * ext[PAD - 2 : PAD - 2 + rows, :]
        )


def ahead_kernel(weight_hbm, weight_ref, sems):
    for one in fetch_weight(weight_hbm, weight_ref, sems, weight_hbm.shape[1] - RIGHT_TILES * COLUMN_TILE):
        one.wait()


def project(mixed, weight_buf, fetched, outs):
    piece = mixed.shape[0] // len(outs)
    tiles, _, width = weight_buf.shape
    for i in range(tiles):
        if fetched is not None:
            fetched[i].wait()
        where = slice(i * width, (i + 1) * width)
        product = jnp.dot(mixed[...], weight_buf[i], preferred_element_type=F32)
        for place, out in enumerate(outs):
            out[:, where] = product[place * piece : (place + 1) * piece].astype(out.dtype)


def across_kernel(
    place_ref, local_ref, query_ref, after_ref, fix_ref, rate_ref, residue_ref, weight_ref,
    right_two, right_three, mixed_ref,
    coef,
):
    mix(place_ref, local_ref, query_ref, after_ref, fix_ref, rate_ref, residue_ref, mixed_ref, coef)
    project(mixed_ref, weight_ref, None, [right_two, right_three])


def left_kernel(mixed_ref, weight_hbm, left_two, left_three, weight_buf, sems):
    fetched = fetch_weight(weight_hbm, weight_buf, sems, 0)
    project(mixed_ref, weight_buf, fetched, [left_two, left_three])


def own_kernel(
    place_ref, local_ref, query_ref, after_ref, fix_ref, rate_ref, residue_ref, weight_hbm,
    beside_ref, own_ref,
    mixed, coef, weight_buf, sems,
):
    fetched = fetch_weight(weight_hbm, weight_buf, sems, 0)
    mix(place_ref, local_ref, query_ref, after_ref, fix_ref, rate_ref, residue_ref, mixed, coef)
    project(mixed, weight_buf, fetched, [beside_ref, own_ref])


def mix(place_ref, local_ref, query_ref, after_ref, fix_ref, rate_ref, residue_ref, mixed, coef):
    half_rows = mixed.shape[0]
    piece = half_rows // 2
    base = place_ref[0]
    swap = place_ref[1]
    before = (base - 1).astype(F32)
    coef[...] = residue_ref[...] * after_ref[...] * jnp.exp(-rate_ref[...] * before)
    phase = lax.broadcasted_iota(jnp.int32, (SUB, LANES), 0)
    at_start = base == 0
    row_zero = jnp.logical_and(phase == 0, at_start)
    row_one = jnp.logical_and(phase == 1, at_start)
    zero = jnp.zeros((SUB, LANES), F32)
    for group in range(SUB):
        lanes = slice(group * LANES, (group + 1) * LANES)
        carry, decay = [], []
        for m in range(MODES):
            line = slice(m * SUB + group, m * SUB + group + 1)
            rate = rate_ref[line, :]
            carry.append(jnp.exp(-rate * phase.astype(F32)) * coef[line, :])
            decay.append(jnp.broadcast_to(jnp.exp(-rate * float(SUB)), (SUB, LANES)))

        def fix(i):
            return jnp.broadcast_to(fix_ref[i * SUB + group : i * SUB + group + 1, :], (SUB, LANES))

        for tile in range(0, half_rows, 2 * SUB):
            parts = []
            for inner in range(2):
                offset = tile + inner * SUB
                spot = pl.ds(pl.multiple_of(base + offset, SUB), SUB)
                carried = summed(carry)
                query = query_ref[spot, lanes]
                if offset == 0:
                    carried = jnp.where(row_zero, fix(0), carried) + jnp.where(row_one, fix(1), zero)
                    query = query + jnp.where(row_zero, fix(2), zero) + jnp.where(row_one, fix(3), zero)
                parts.append((local_ref[spot, lanes] + carried) * query)
                carry = [carry[m] * decay[m] for m in range(MODES)]
            block = tile // piece
            row = pl.multiple_of((block ^ swap) * piece + tile % piece, 2 * SUB)
            mixed[pl.ds(row, 2 * SUB), lanes] = jnp.concatenate(parts, axis=0).astype(BF16)


def scan_states(payload, sent, rate, taps, rows, place, count, beside):
    tap = taps.reshape(3, SHORT, SUB, LANES)

    def head_gated(tail, head):
        def filtered(s, first, second, older, newer):
            return (
                tap[s][0] * first + tap[s][1] * newer + tap[s][2] * older,
                tap[s][0] * second + tap[s][1] * first + tap[s][2] * newer,
            )

        keys = filtered(1, head[0], head[1], tail[2], tail[3])
        values = filtered(2, head[2], head[3], tail[4], tail[5])
        return [(k * v).astype(BF16).astype(F32) for k, v in zip(keys, values, strict=True)]

    def decayed(steps):
        return jnp.exp(-rate * steps)

    def joined(pair):
        return decayed(1.0) * pair[0] + pair[1]

    mine = payload.reshape(-1, SUB, LANES)
    own_head = mine[MODES : MODES + HEADS]
    total, head, tail = mine[:MODES], own_head, mine[MODES + HEADS :]
    start = jnp.zeros_like(total)
    border = jnp.zeros_like(tail)
    bits = (count - 1).bit_length()
    for bit in range(bits):
        width = 1 << bit
        mask = width
        if bit >= 2 and bit % 2 == 0 and bit < bits:
            mask = width | (width >> 1)
        sent = beside(bit, sent)
        got = lax.ppermute(sent, "seq", [(j, j ^ mask) for j in range(count)])
        theirs = got.reshape(-1, SUB, LANES).astype(F32)
        upper = ((place >> bit) & 1) == 1
        low = place % width
        length = rows * width
        other_total, other_head, other_tail = theirs[:MODES], theirs[MODES : MODES + HEADS], theirs[MODES + HEADS :]
        low_total = jnp.where(upper, other_total, total)
        low_tail = jnp.where(upper, other_tail, tail)
        high_head = jnp.where(upper, head, other_head)
        entry = joined(head_gated(low_tail, high_head))
        gone = (rows * low).astype(F32)
        start = start + jnp.where(
            upper,
            decayed(gone) * other_total
            + jnp.where(low > 0, decayed(jnp.maximum(gone - 2.0, 0.0)) * entry, 0.0),
            0.0,
        )
        border = jnp.where(jnp.logical_and(upper, low == 0), other_tail, border)
        if bit < bits - 1:
            high_total = jnp.where(upper, total, other_total)
            total = decayed(float(length)) * low_total + high_total + decayed(float(length - 2)) * entry
            tail = jnp.where(upper, tail, other_tail)
        head = jnp.where(upper, other_head, head)
        if bit < bits - 1:
            sent = jnp.concatenate([total, head, tail]).reshape(-1, LANES).astype(BF16)
    first = joined(head_gated(jnp.zeros_like(border), head))
    gone = (rows * place).astype(F32)
    start = start + jnp.where(place > 0, decayed(jnp.maximum(gone - 2.0, 0.0)) * first, 0.0)
    return start, border, head_gated(border, own_head), tap


def on_device(query_stream, key_stream, value_stream, short_filter, decay_rate, residues, skip_bias, out_weight):
    rows, channels = query_stream.shape
    assert channels == SUB * LANES
    columns = out_weight.shape[1]
    pitch = rows + PAD
    count = lax.axis_size("seq")
    place = lax.axis_index("seq")
    parts = lax.axis_size("chan")
    mine = lax.axis_index("chan")
    assert parts == 4
    piece = rows // parts
    query_stream, key_stream, value_stream, short_filter, out_weight, rates, residues, skips = (
        pltpu.with_memory_space_constraint(array, pltpu.HBM)
        for array in (
            query_stream, key_stream, value_stream, short_filter, out_weight,
            decay_rate.T, residues.T, skip_bias.reshape(SUB, LANES),
        )
    )
    params = pltpu.CompilerParams(vmem_limit_bytes=VMEM_LIMIT)
    dma = pltpu.SemaphoreType.DMA
    payload, sent, rate, gated, taps, residue, skip = pl.pallas_call(
        state_kernel,
        out_shape=(
            jax.ShapeDtypeStruct((PAYLOAD, LANES), F32),
            jax.ShapeDtypeStruct((PAYLOAD, LANES), BF16),
            jax.ShapeDtypeStruct((STATE_ROWS, LANES), F32),
            jax.ShapeDtypeStruct((SUB * pitch, LANES), F32),
            jax.ShapeDtypeStruct((3 * SHORT * SUB, LANES), F32),
            jax.ShapeDtypeStruct((STATE_ROWS, LANES), F32),
            jax.ShapeDtypeStruct((SUB, LANES), F32),
        ),
        in_specs=[HBM] * 7,
        out_specs=(VMEM,) * 7,
        scratch_shapes=[
            pltpu.VMEM((rows, channels), BF16),
            pltpu.VMEM((rows, channels), BF16),
            pltpu.VMEM((16, channels), BF16),
            pltpu.VMEM((3, SHORT, channels), F32),
            pltpu.VMEM((MODES, channels), F32),
            pltpu.VMEM((MODES, channels), F32),
            pltpu.VMEM((pitch, LANES), F32),
            pltpu.VMEM((pitch, LANES), F32),
            dma((5 + 2 * CUTS,)),
        ],
        compiler_params=params,
        cost_estimate=pl.CostEstimate(flops=20_000_000, bytes_accessed=3_000_000, transcendentals=0),
    )(query_stream, key_stream, value_stream, short_filter, rates, residues, skips)
    right_side = RIGHT_TILES * COLUMN_TILE
    left_side = columns - right_side
    aside = {}

    light = pl.CostEstimate(flops=1_000_000, bytes_accessed=100_000, transcendentals=0)

    def local_part(gated):
        return pl.pallas_call(
            local_kernel,
            out_shape=jax.ShapeDtypeStruct((rows, channels), F32),
            in_specs=[VMEM] * 4,
            out_specs=VMEM,
            scratch_shapes=[pltpu.VMEM((SUB * pitch, LANES), F32)],
            compiler_params=params,
            cost_estimate=light,
        )(gated, rate, residue, skip)

    def query_part(taps):
        return pl.pallas_call(
            query_kernel,
            out_shape=jax.ShapeDtypeStruct((rows, channels), F32),
            in_specs=[HBM, VMEM],
            out_specs=VMEM,
            scratch_shapes=[
                pltpu.VMEM((rows, channels), BF16),
                pltpu.VMEM((pitch, LANES), F32),
                dma((1,)),
            ],
            compiler_params=params,
            cost_estimate=pl.CostEstimate(flops=1_000_000, bytes_accessed=100_000, transcendentals=0),
        )(query_stream, taps)

    def weight_part(out_weight):
        return pl.pallas_call(
            ahead_kernel,
            out_shape=jax.ShapeDtypeStruct((RIGHT_TILES, channels, COLUMN_TILE), BF16),
            in_specs=[HBM],
            out_specs=VMEM,
            scratch_shapes=[dma((RIGHT_TILES,))],
            compiler_params=params,
            cost_estimate=light,
        )(out_weight)

    def beside_scan(bit, sent):
        last = (count - 1).bit_length() - 1
        if bit == last - 2:
            sent, aside["local"] = lax.optimization_barrier((sent, gated))
        elif bit == last - 1:
            aside["local"] = local_part(aside["local"])
            sent, aside["local"], aside["query"] = lax.optimization_barrier((sent, aside["local"], taps))
        elif bit == last:
            aside["query"] = query_part(aside["query"])
            sent, aside["query"], weight = lax.optimization_barrier((sent, aside["query"], out_weight))
            aside["right"] = weight_part(weight)
        return sent

    rate_rows = rate.reshape(MODES, SUB, LANES)
    start, border, gates, tap = scan_states(payload, sent, rate_rows, taps, rows, place, count, beside_scan)
    local = aside["local"]
    query = aside["query"]
    residue_rows = residue.reshape(MODES, SUB, LANES)
    after_zero = jnp.exp(-rate_rows) * start + gates[0]
    after_one = jnp.exp(-rate_rows) * after_zero + gates[1]
    fixes = jnp.concatenate(
        [
            jnp.sum(residue_rows * after_zero, axis=0) + skip * gates[0],
            skip * gates[1],
            tap[0][1] * border[1] + tap[0][2] * border[0],
            tap[0][2] * border[1],
        ]
    )

    def half_inputs(half, swap):
        at = jnp.stack([half * 2 * piece, swap]).astype(jnp.int32)
        return at, local, query, after_one.reshape(STATE_ROWS, LANES), fixes, rate, residue

    def sent_by(block, pairs):
        return lax.ppermute(block, "chan", pairs)

    def across(step):
        return [(j, j ^ step) for j in range(parts)]

    own_half, odd = mine // 2, mine % 2
    right_two, right_three, mixed = pl.pallas_call(
        across_kernel,
        out_shape=(
            jax.ShapeDtypeStruct((piece, right_side), BF16),
            jax.ShapeDtypeStruct((piece, right_side), BF16),
            jax.ShapeDtypeStruct((2 * piece, channels), BF16),
        ),
        in_specs=[SMEM] + [VMEM] * 7,
        out_specs=(VMEM,) * 3,
        scratch_shapes=[pltpu.VMEM((STATE_ROWS, LANES), F32)],
        compiler_params=params,
        cost_estimate=light,
    )(*half_inputs(1 - own_half, odd), aside["right"])
    left_tiles, tiles = left_side // COLUMN_TILE, columns // COLUMN_TILE
    left_two, left_three = pl.pallas_call(
        left_kernel,
        out_shape=(jax.ShapeDtypeStruct((piece, left_side), BF16),) * 2,
        in_specs=[VMEM, HBM],
        out_specs=(VMEM,) * 2,
        scratch_shapes=[pltpu.VMEM((left_tiles, channels, COLUMN_TILE), BF16), dma((left_tiles,))],
        compiler_params=params,
        cost_estimate=light,
    )(mixed, out_weight)
    handed_three = sent_by(right_three, [(0, 1), (3, 2)])
    handed_two = sent_by(right_two, [(0, 1), (3, 2)])
    got_two, got_three = sent_by(left_two, across(2)), sent_by(left_three, across(3))
    beside, own = pl.pallas_call(
        own_kernel,
        out_shape=(
            jax.ShapeDtypeStruct((piece, columns), BF16),
            jax.ShapeDtypeStruct((piece, columns), F32),
        ),
        in_specs=[SMEM] + [VMEM] * 6 + [HBM],
        out_specs=(VMEM,) * 2,
        scratch_shapes=[
            pltpu.VMEM((2 * piece, channels), BF16),
            pltpu.VMEM((STATE_ROWS, LANES), F32),
            pltpu.VMEM((tiles, channels, COLUMN_TILE), BF16),
            dma((tiles,)),
        ],
        compiler_params=params,
        cost_estimate=light,
    )(*half_inputs(own_half, 1 - odd), out_weight)
    got_one = sent_by(beside, across(1))
    handed_three, _ = lax.optimization_barrier((handed_three, beside))
    joined_two = (right_two.astype(F32) + handed_three.astype(F32)).astype(BF16)
    handed_two, _ = lax.optimization_barrier((handed_two, joined_two))
    joined_three = (right_three.astype(F32) + handed_two.astype(F32)).astype(BF16)
    far_two = sent_by(joined_two, [(1, 3), (2, 0)])
    far_three = sent_by(joined_three, [(1, 2), (2, 1)])
    left = got_two.astype(F32) + got_three.astype(F32)
    far = far_two.astype(F32) + far_three.astype(F32)
    total = own + got_one.astype(F32) + jnp.concatenate([left, far], axis=1)
    return total.astype(BF16)


def solution(mesh):
    return jax.shard_map(
        on_device,
        mesh=mesh,
        in_specs=(
            P("seq", "chan"),
            P("seq", "chan"),
            P("seq", "chan"),
            P(None, None, "chan"),
            P("chan", None),
            P("chan", None),
            P("chan"),
            P("chan", None),
        ),
        out_specs=P(("seq", "chan"), None),
        check_vma=False,
    )
```

```python
import jax
import jax.numpy as jnp
from jax import lax
from jax.experimental import pallas as pl
from jax.experimental.pallas import tpu as pltpu
from jax.sharding import PartitionSpec as P

MODES = 16
SHORT = 3
F32 = jnp.float32
BF16 = jnp.bfloat16
LANES = 128
SUB = 8
PAD = 8
STATE_ROWS = MODES * SUB
HEADS = 4
TAILS = 6
PAYLOAD = STATE_ROWS + SUB * (HEADS + TAILS)
COLUMN_TILE = 512
RIGHT_TILES = 5
CUTS = 4
VMEM_LIMIT = 20 * 1024 * 1024
HBM = pl.BlockSpec(memory_space=pltpu.HBM)
VMEM = pl.BlockSpec(memory_space=pltpu.VMEM)
SMEM = pl.BlockSpec(memory_space=pltpu.SMEM)


def summed(terms):
    terms = list(terms)
    while len(terms) > 1:
        terms = [terms[i] + terms[i + 1] for i in range(0, len(terms), 2)]
    return terms[0]


def short_taps(ext, taps_ref, stream, lanes, count):
    return (
        taps_ref[stream, 0:1, lanes] * ext[PAD : PAD + count, :]
        + taps_ref[stream, 1:2, lanes] * ext[PAD - 1 : PAD - 1 + count, :]
        + taps_ref[stream, 2:3, lanes] * ext[PAD - 2 : PAD - 2 + count, :]
    )


def to_rows(source, target):
    for group in range(SUB):
        target[pl.ds(group, MODES, stride=SUB), :] = source[:, group * LANES : (group + 1) * LANES]


def copies(pairs, sems):
    made = [pltpu.make_async_copy(a, b, sems.at[i]) for i, (a, b) in enumerate(pairs)]
    for one in made:
        one.start()
    return made


def fetch_weight(weight_hbm, weight_buf, sems, first):
    tiles, _, width = weight_buf.shape
    made = [
        pltpu.make_async_copy(weight_hbm.at[:, pl.ds(first + i * width, width)], weight_buf.at[i], sems.at[i])
        for i in range(tiles)
    ]
    for one in made:
        one.start()
    return made


def state_kernel(
    query_hbm, key_hbm, value_hbm, taps_hbm, rate_hbm, residue_hbm, skip_hbm,
    payload_ref, sent_ref, rate_ref, gated_ref, taps_ref, residue_ref, skip_ref,
    key_buf, value_buf, query_buf, taps_buf, rate_buf, residue_buf, ext_key, ext_value, sems,
):
    rows, channels = key_buf.shape
    pitch = rows + PAD
    width = channels // CUTS
    made = copies(
        [(rate_hbm, rate_buf), (taps_hbm, taps_buf)]
        + [
            (hbm.at[:, pl.ds(part * width, width)], buf.at[:, pl.ds(part * width, width)])
            for part in range(CUTS)
            for hbm, buf in ((key_hbm, key_buf), (value_hbm, value_buf))
        ]
        + [(query_hbm.at[pl.ds(rows - 16, 16), :], query_buf), (residue_hbm, residue_buf), (skip_hbm, skip_ref)],
        sems,
    )
    ext_key[0:PAD, :] = jnp.zeros((PAD, LANES), F32)
    ext_value[0:PAD, :] = jnp.zeros((PAD, LANES), F32)
    made[0].wait()
    to_rows(rate_buf, rate_ref)
    made[1].wait()
    for group in range(SUB):
        if group % (SUB // CUTS) == 0:
            part = group // (SUB // CUTS)
            made[2 + 2 * part].wait()
            made[3 + 2 * part].wait()
        lanes = slice(group * LANES, (group + 1) * LANES)
        ext_key[PAD : PAD + rows, :] = key_buf[:, lanes].astype(F32)
        ext_value[PAD : PAD + rows, :] = value_buf[:, lanes].astype(F32)
        gated = short_taps(ext_key, taps_buf, 1, lanes, rows) * short_taps(ext_value, taps_buf, 2, lanes, rows)
        base = group * pitch
        gated_ref[base : base + rows, :] = gated.astype(BF16).astype(F32)
        gated_ref[base : base + 2, :] = jnp.zeros((2, LANES), F32)
        gated_ref[base + rows : base + pitch, :] = jnp.zeros((PAD, LANES), F32)
        for place, (ext, row) in enumerate(
            ((ext_key, 0), (ext_key, 1), (ext_value, 0), (ext_value, 1))
        ):
            at = STATE_ROWS + place * SUB + group
            payload_ref[at : at + 1, :] = ext[PAD + row : PAD + row + 1, :]
        for place, (ext, row) in enumerate(
            ((ext_key, rows - 2), (ext_key, rows - 1), (ext_value, rows - 2), (ext_value, rows - 1))
        ):
            at = STATE_ROWS + (HEADS + 2 + place) * SUB + group
            payload_ref[at : at + 1, :] = ext[PAD + row : PAD + row + 1, :]
    decay = [jnp.exp(-rate_ref[m * SUB : (m + 1) * SUB, :]) for m in range(MODES)]

    def step(t, carry):
        now = gated_ref[pl.ds(t, SUB, stride=pitch), :]
        return tuple(decay[m] * carry[m] + now for m in range(MODES))

    final = lax.fori_loop(0, rows, step, tuple(jnp.zeros((SUB, LANES), F32) for _ in range(MODES)), unroll=8)
    for m in range(MODES):
        payload_ref[m * SUB : (m + 1) * SUB, :] = final[m]
    for one in made[2 + 2 * CUTS :]:
        one.wait()
    to_rows(residue_buf, residue_ref)
    last = query_buf[...].astype(F32)
    for place, row in enumerate((14, 15)):
        for group in range(SUB):
            at = STATE_ROWS + (HEADS + place) * SUB + group
            payload_ref[at : at + 1, :] = last[row : row + 1, group * LANES : (group + 1) * LANES]
    sent_ref[...] = payload_ref[...].astype(BF16)
    for stream in range(3):
        for tap in range(SHORT):
            for group in range(SUB):
                at = (stream * SHORT + tap) * SUB + group
                taps_ref[at : at + 1, :] = taps_buf[stream, tap : tap + 1, group * LANES : (group + 1) * LANES]


def local_kernel(gated_ref, rate_ref, residue_ref, skip_ref, local_ref, conv):
    rows = local_ref.shape[0]
    pitch = rows + PAD
    decay = [jnp.exp(-rate_ref[m * SUB : (m + 1) * SUB, :]) for m in range(MODES)]

    def step(t, carry):
        now = gated_ref[pl.ds(t, SUB, stride=pitch), :]
        fresh = tuple(decay[m] * carry[m] + now for m in range(MODES))
        conv[pl.ds(t, SUB, stride=pitch), :] = summed(
            residue_ref[m * SUB : (m + 1) * SUB, :] * fresh[m] for m in range(MODES)
        )
        return fresh

    lax.fori_loop(0, rows, step, tuple(jnp.zeros((SUB, LANES), F32) for _ in range(MODES)), unroll=8)
    for group in range(SUB):
        lanes = slice(group * LANES, (group + 1) * LANES)
        spot = slice(group * pitch, group * pitch + rows)
        local_ref[:, lanes] = conv[spot, :] + skip_ref[group : group + 1, :] * gated_ref[spot, :]


def query_kernel(query_hbm, taps_ref, query_ref, query_buf, ext, sems):
    rows = query_ref.shape[0]
    made = copies([(query_hbm, query_buf)], sems)
    ext[0:PAD, :] = jnp.zeros((PAD, LANES), F32)
    made[0].wait()
    for group in range(SUB):
        lanes = slice(group * LANES, (group + 1) * LANES)
        ext[PAD : PAD + rows, :] = query_buf[:, lanes].astype(F32)
        tap = [taps_ref[p * SUB + group : p * SUB + group + 1, :] for p in range(SHORT)]
        query_ref[:, lanes] = (
            tap[0] * ext[PAD : PAD + rows, :]
            + tap[1] * ext[PAD - 1 : PAD - 1 + rows, :]
            + tap[2] * ext[PAD - 2 : PAD - 2 + rows, :]
        )


def ahead_kernel(weight_hbm, weight_ref, sems):
    for one in fetch_weight(weight_hbm, weight_ref, sems, weight_hbm.shape[1] - RIGHT_TILES * COLUMN_TILE):
        one.wait()


def project(mixed, weight_buf, fetched, outs):
    piece = mixed.shape[0] // len(outs)
    tiles, _, width = weight_buf.shape
    for i in range(tiles):
        if fetched is not None:
            fetched[i].wait()
        where = slice(i * width, (i + 1) * width)
        product = jnp.dot(mixed[...], weight_buf[i], preferred_element_type=F32)
        for place, out in enumerate(outs):
            out[:, where] = product[place * piece : (place + 1) * piece].astype(out.dtype)


def across_kernel(
    place_ref, local_ref, query_ref, after_ref, fix_ref, rate_ref, residue_ref, weight_ref,
    right_ref, mixed_ref,
    coef,
):
    mix(place_ref, local_ref, query_ref, after_ref, fix_ref, rate_ref, residue_ref, mixed_ref, coef)
    project(mixed_ref, weight_ref, None, [right_ref])


def left_kernel(mixed_ref, weight_hbm, left_two, left_three, weight_buf, sems):
    fetched = fetch_weight(weight_hbm, weight_buf, sems, 0)
    project(mixed_ref, weight_buf, fetched, [left_two, left_three])


def own_kernel(
    place_ref, local_ref, query_ref, after_ref, fix_ref, rate_ref, residue_ref, weight_hbm,
    beside_ref, own_ref,
    mixed, coef, weight_buf, sems,
):
    fetched = fetch_weight(weight_hbm, weight_buf, sems, 0)
    mix(place_ref, local_ref, query_ref, after_ref, fix_ref, rate_ref, residue_ref, mixed, coef)
    project(mixed, weight_buf, fetched, [beside_ref, own_ref])


def mix(place_ref, local_ref, query_ref, after_ref, fix_ref, rate_ref, residue_ref, mixed, coef):
    half_rows = mixed.shape[0]
    piece = half_rows // 2
    base = place_ref[0]
    swap = place_ref[1]
    before = (base - 1).astype(F32)
    coef[...] = residue_ref[...] * after_ref[...] * jnp.exp(-rate_ref[...] * before)
    phase = lax.broadcasted_iota(jnp.int32, (SUB, LANES), 0)
    at_start = base == 0
    row_zero = jnp.logical_and(phase == 0, at_start)
    row_one = jnp.logical_and(phase == 1, at_start)
    zero = jnp.zeros((SUB, LANES), F32)
    for group in range(SUB):
        lanes = slice(group * LANES, (group + 1) * LANES)
        carry, decay = [], []
        for m in range(MODES):
            line = slice(m * SUB + group, m * SUB + group + 1)
            rate = rate_ref[line, :]
            carry.append(jnp.exp(-rate * phase.astype(F32)) * coef[line, :])
            decay.append(jnp.broadcast_to(jnp.exp(-rate * float(SUB)), (SUB, LANES)))

        def fix(i):
            return jnp.broadcast_to(fix_ref[i * SUB + group : i * SUB + group + 1, :], (SUB, LANES))

        for tile in range(0, half_rows, 2 * SUB):
            parts = []
            for inner in range(2):
                offset = tile + inner * SUB
                spot = pl.ds(pl.multiple_of(base + offset, SUB), SUB)
                carried = summed(carry)
                query = query_ref[spot, lanes]
                if offset == 0:
                    carried = jnp.where(row_zero, fix(0), carried) + jnp.where(row_one, fix(1), zero)
                    query = query + jnp.where(row_zero, fix(2), zero) + jnp.where(row_one, fix(3), zero)
                parts.append((local_ref[spot, lanes] + carried) * query)
                carry = [carry[m] * decay[m] for m in range(MODES)]
            block = tile // piece
            row = pl.multiple_of((block ^ swap) * piece + tile % piece, 2 * SUB)
            mixed[pl.ds(row, 2 * SUB), lanes] = jnp.concatenate(parts, axis=0).astype(BF16)


def scan_states(payload, sent, rate, taps, rows, place, count, beside):
    tap = taps.reshape(3, SHORT, SUB, LANES)

    def head_gated(tail, head):
        def filtered(s, first, second, older, newer):
            return (
                tap[s][0] * first + tap[s][1] * newer + tap[s][2] * older,
                tap[s][0] * second + tap[s][1] * first + tap[s][2] * newer,
            )

        keys = filtered(1, head[0], head[1], tail[2], tail[3])
        values = filtered(2, head[2], head[3], tail[4], tail[5])
        return [(k * v).astype(BF16).astype(F32) for k, v in zip(keys, values, strict=True)]

    def decayed(steps):
        return jnp.exp(-rate * steps)

    def joined(pair):
        return decayed(1.0) * pair[0] + pair[1]

    mine = payload.reshape(-1, SUB, LANES)
    own_head = mine[MODES : MODES + HEADS]
    total, head, tail = mine[:MODES], own_head, mine[MODES + HEADS :]
    start = jnp.zeros_like(total)
    border = jnp.zeros_like(tail)
    bits = (count - 1).bit_length()
    for bit in range(bits):
        width = 1 << bit
        mask = width
        if bit >= 2 and bit % 2 == 0 and bit < bits:
            mask = width | (width >> 1)
        sent = beside(bit, sent)
        got = lax.ppermute(sent, "seq", [(j, j ^ mask) for j in range(count)])
        theirs = got.reshape(-1, SUB, LANES).astype(F32)
        upper = ((place >> bit) & 1) == 1
        low = place % width
        length = rows * width
        other_total, other_head, other_tail = theirs[:MODES], theirs[MODES : MODES + HEADS], theirs[MODES + HEADS :]
        low_total = jnp.where(upper, other_total, total)
        low_tail = jnp.where(upper, other_tail, tail)
        high_head = jnp.where(upper, head, other_head)
        entry = joined(head_gated(low_tail, high_head))
        gone = (rows * low).astype(F32)
        start = start + jnp.where(
            upper,
            decayed(gone) * other_total
            + jnp.where(low > 0, decayed(jnp.maximum(gone - 2.0, 0.0)) * entry, 0.0),
            0.0,
        )
        border = jnp.where(jnp.logical_and(upper, low == 0), other_tail, border)
        if bit < bits - 1:
            high_total = jnp.where(upper, total, other_total)
            total = decayed(float(length)) * low_total + high_total + decayed(float(length - 2)) * entry
            tail = jnp.where(upper, tail, other_tail)
        head = jnp.where(upper, other_head, head)
        if bit < bits - 1:
            sent = jnp.concatenate([total, head, tail]).reshape(-1, LANES).astype(BF16)
    first = joined(head_gated(jnp.zeros_like(border), head))
    gone = (rows * place).astype(F32)
    start = start + jnp.where(place > 0, decayed(jnp.maximum(gone - 2.0, 0.0)) * first, 0.0)
    return start, border, head_gated(border, own_head), tap


def on_device(query_stream, key_stream, value_stream, short_filter, decay_rate, residues, skip_bias, out_weight):
    rows, channels = query_stream.shape
    assert channels == SUB * LANES
    columns = out_weight.shape[1]
    pitch = rows + PAD
    count = lax.axis_size("seq")
    place = lax.axis_index("seq")
    parts = lax.axis_size("chan")
    mine = lax.axis_index("chan")
    assert parts == 4
    piece = rows // parts
    query_stream, key_stream, value_stream, short_filter, out_weight, rates, residues, skips = (
        pltpu.with_memory_space_constraint(array, pltpu.HBM)
        for array in (
            query_stream, key_stream, value_stream, short_filter, out_weight,
            decay_rate.T, residues.T, skip_bias.reshape(SUB, LANES),
        )
    )
    params = pltpu.CompilerParams(vmem_limit_bytes=VMEM_LIMIT)
    dma = pltpu.SemaphoreType.DMA
    payload, sent, rate, gated, taps, residue, skip = pl.pallas_call(
        state_kernel,
        out_shape=(
            jax.ShapeDtypeStruct((PAYLOAD, LANES), F32),
            jax.ShapeDtypeStruct((PAYLOAD, LANES), BF16),
            jax.ShapeDtypeStruct((STATE_ROWS, LANES), F32),
            jax.ShapeDtypeStruct((SUB * pitch, LANES), F32),
            jax.ShapeDtypeStruct((3 * SHORT * SUB, LANES), F32),
            jax.ShapeDtypeStruct((STATE_ROWS, LANES), F32),
            jax.ShapeDtypeStruct((SUB, LANES), F32),
        ),
        in_specs=[HBM] * 7,
        out_specs=(VMEM,) * 7,
        scratch_shapes=[
            pltpu.VMEM((rows, channels), BF16),
            pltpu.VMEM((rows, channels), BF16),
            pltpu.VMEM((16, channels), BF16),
            pltpu.VMEM((3, SHORT, channels), F32),
            pltpu.VMEM((MODES, channels), F32),
            pltpu.VMEM((MODES, channels), F32),
            pltpu.VMEM((pitch, LANES), F32),
            pltpu.VMEM((pitch, LANES), F32),
            dma((5 + 2 * CUTS,)),
        ],
        compiler_params=params,
        cost_estimate=pl.CostEstimate(flops=20_000_000, bytes_accessed=3_000_000, transcendentals=0),
    )(query_stream, key_stream, value_stream, short_filter, rates, residues, skips)
    right_side = RIGHT_TILES * COLUMN_TILE
    left_side = columns - right_side
    aside = {}

    light = pl.CostEstimate(flops=1_000_000, bytes_accessed=100_000, transcendentals=0)

    def local_part(gated):
        return pl.pallas_call(
            local_kernel,
            out_shape=jax.ShapeDtypeStruct((rows, channels), F32),
            in_specs=[VMEM] * 4,
            out_specs=VMEM,
            scratch_shapes=[pltpu.VMEM((SUB * pitch, LANES), F32)],
            compiler_params=params,
            cost_estimate=light,
        )(gated, rate, residue, skip)

    def query_part(taps):
        return pl.pallas_call(
            query_kernel,
            out_shape=jax.ShapeDtypeStruct((rows, channels), F32),
            in_specs=[HBM, VMEM],
            out_specs=VMEM,
            scratch_shapes=[
                pltpu.VMEM((rows, channels), BF16),
                pltpu.VMEM((pitch, LANES), F32),
                dma((1,)),
            ],
            compiler_params=params,
            cost_estimate=pl.CostEstimate(flops=1_000_000, bytes_accessed=100_000, transcendentals=0),
        )(query_stream, taps)

    def weight_part(out_weight):
        return pl.pallas_call(
            ahead_kernel,
            out_shape=jax.ShapeDtypeStruct((RIGHT_TILES, channels, COLUMN_TILE), BF16),
            in_specs=[HBM],
            out_specs=VMEM,
            scratch_shapes=[dma((RIGHT_TILES,))],
            compiler_params=params,
            cost_estimate=light,
        )(out_weight)

    def beside_scan(bit, sent):
        last = (count - 1).bit_length() - 1
        if bit == last - 2:
            sent, aside["local"] = lax.optimization_barrier((sent, gated))
        elif bit == last - 1:
            aside["local"] = local_part(aside["local"])
            sent, aside["local"], aside["query"] = lax.optimization_barrier((sent, aside["local"], taps))
        elif bit == last:
            aside["query"] = query_part(aside["query"])
            sent, aside["query"], weight = lax.optimization_barrier((sent, aside["query"], out_weight))
            aside["right"] = weight_part(weight)
        return sent

    rate_rows = rate.reshape(MODES, SUB, LANES)
    start, border, gates, tap = scan_states(payload, sent, rate_rows, taps, rows, place, count, beside_scan)
    local = aside["local"]
    query = aside["query"]
    residue_rows = residue.reshape(MODES, SUB, LANES)
    after_zero = jnp.exp(-rate_rows) * start + gates[0]
    after_one = jnp.exp(-rate_rows) * after_zero + gates[1]
    fixes = jnp.concatenate(
        [
            jnp.sum(residue_rows * after_zero, axis=0) + skip * gates[0],
            skip * gates[1],
            tap[0][1] * border[1] + tap[0][2] * border[0],
            tap[0][2] * border[1],
        ]
    )

    def half_inputs(half, swap):
        at = jnp.stack([half * 2 * piece, swap]).astype(jnp.int32)
        return at, local, query, after_one.reshape(STATE_ROWS, LANES), fixes, rate, residue

    def sent_by(block, pairs):
        return lax.ppermute(block, "chan", pairs)

    def across(step):
        return [(j, j ^ step) for j in range(parts)]

    own_half, odd = mine // 2, mine % 2
    right, mixed = pl.pallas_call(
        across_kernel,
        out_shape=(
            jax.ShapeDtypeStruct((2 * piece, right_side), BF16),
            jax.ShapeDtypeStruct((2 * piece, channels), BF16),
        ),
        in_specs=[SMEM] + [VMEM] * 7,
        out_specs=(VMEM,) * 2,
        scratch_shapes=[pltpu.VMEM((STATE_ROWS, LANES), F32)],
        compiler_params=params,
        cost_estimate=light,
    )(*half_inputs(1 - own_half, odd), aside["right"])
    left_tiles, tiles = left_side // COLUMN_TILE, columns // COLUMN_TILE
    left_two, left_three = pl.pallas_call(
        left_kernel,
        out_shape=(jax.ShapeDtypeStruct((piece, left_side), BF16),) * 2,
        in_specs=[VMEM, HBM],
        out_specs=(VMEM,) * 2,
        scratch_shapes=[pltpu.VMEM((left_tiles, channels, COLUMN_TILE), BF16), dma((left_tiles,))],
        compiler_params=params,
        cost_estimate=light,
    )(mixed, out_weight)
    handed = sent_by(right, [(0, 1), (3, 2)])
    got_two, got_three = sent_by(left_two, across(2)), sent_by(left_three, across(3))
    beside, own = pl.pallas_call(
        own_kernel,
        out_shape=(
            jax.ShapeDtypeStruct((piece, columns), BF16),
            jax.ShapeDtypeStruct((piece, columns), F32),
        ),
        in_specs=[SMEM] + [VMEM] * 6 + [HBM],
        out_specs=(VMEM,) * 2,
        scratch_shapes=[
            pltpu.VMEM((2 * piece, channels), BF16),
            pltpu.VMEM((STATE_ROWS, LANES), F32),
            pltpu.VMEM((tiles, channels, COLUMN_TILE), BF16),
            dma((tiles,)),
        ],
        compiler_params=params,
        cost_estimate=light,
    )(*half_inputs(own_half, 1 - odd), out_weight)
    got_one = sent_by(beside, across(1))
    handed, _ = lax.optimization_barrier((handed, beside))
    joined_two = (right[:piece].astype(F32) + handed[piece:].astype(F32)).astype(BF16)
    joined_three = (right[piece:].astype(F32) + handed[:piece].astype(F32)).astype(BF16)
    far_two = sent_by(joined_two, [(1, 3), (2, 0)])
    far_three = sent_by(joined_three, [(1, 2), (2, 1)])
    left = got_two.astype(F32) + got_three.astype(F32)
    far = far_two.astype(F32) + far_three.astype(F32)
    total = own + got_one.astype(F32) + jnp.concatenate([left, far], axis=1)
    return total.astype(BF16)


def solution(mesh):
    return jax.shard_map(
        on_device,
        mesh=mesh,
        in_specs=(
            P("seq", "chan"),
            P("seq", "chan"),
            P("seq", "chan"),
            P(None, None, "chan"),
            P("chan", None),
            P("chan", None),
            P("chan"),
            P("chan", None),
        ),
        out_specs=P(("seq", "chan"), None),
        check_vma=False,
    )
```

```python
import jax
import jax.numpy as jnp
from jax import lax
from jax.experimental import pallas as pl
from jax.experimental.pallas import tpu as pltpu
from jax.sharding import PartitionSpec as P

MODES = 16
SHORT = 3
F32 = jnp.float32
BF16 = jnp.bfloat16
LANES = 128
SUB = 8
PAD = 8
STATE_ROWS = MODES * SUB
HEADS = 4
TAILS = 6
PAYLOAD = STATE_ROWS + SUB * (HEADS + TAILS)
COLUMN_TILE = 512
RIGHT_TILES = 5
CUTS = 4
VMEM_LIMIT = 20 * 1024 * 1024
HBM = pl.BlockSpec(memory_space=pltpu.HBM)
VMEM = pl.BlockSpec(memory_space=pltpu.VMEM)
SMEM = pl.BlockSpec(memory_space=pltpu.SMEM)


def summed(terms):
    terms = list(terms)
    while len(terms) > 1:
        terms = [terms[i] + terms[i + 1] for i in range(0, len(terms), 2)]
    return terms[0]


def short_taps(ext, taps_ref, stream, lanes, count):
    return (
        taps_ref[stream, 0:1, lanes] * ext[PAD : PAD + count, :]
        + taps_ref[stream, 1:2, lanes] * ext[PAD - 1 : PAD - 1 + count, :]
        + taps_ref[stream, 2:3, lanes] * ext[PAD - 2 : PAD - 2 + count, :]
    )


def to_rows(source, target):
    for group in range(SUB):
        target[pl.ds(group, MODES, stride=SUB), :] = source[:, group * LANES : (group + 1) * LANES]


def copies(pairs, sems):
    made = [pltpu.make_async_copy(a, b, sems.at[i]) for i, (a, b) in enumerate(pairs)]
    for one in made:
        one.start()
    return made


def fetch_weight(weight_hbm, weight_buf, sems, first):
    tiles, _, width = weight_buf.shape
    made = [
        pltpu.make_async_copy(weight_hbm.at[:, pl.ds(first + i * width, width)], weight_buf.at[i], sems.at[i])
        for i in range(tiles)
    ]
    for one in made:
        one.start()
    return made


def state_kernel(
    query_hbm, key_hbm, value_hbm, taps_hbm, rate_hbm, residue_hbm, skip_hbm,
    payload_ref, sent_ref, rate_ref, gated_ref, taps_ref, residue_ref, skip_ref,
    key_buf, value_buf, query_buf, taps_buf, rate_buf, residue_buf, ext_key, ext_value, sems,
):
    rows, channels = key_buf.shape
    pitch = rows + PAD
    width = channels // CUTS
    made = copies(
        [(rate_hbm, rate_buf), (taps_hbm, taps_buf)]
        + [
            (hbm.at[:, pl.ds(part * width, width)], buf.at[:, pl.ds(part * width, width)])
            for part in range(CUTS)
            for hbm, buf in ((key_hbm, key_buf), (value_hbm, value_buf))
        ]
        + [(query_hbm.at[pl.ds(rows - 16, 16), :], query_buf), (residue_hbm, residue_buf), (skip_hbm, skip_ref)],
        sems,
    )
    ext_key[0:PAD, :] = jnp.zeros((PAD, LANES), F32)
    ext_value[0:PAD, :] = jnp.zeros((PAD, LANES), F32)
    made[0].wait()
    to_rows(rate_buf, rate_ref)
    made[1].wait()
    for group in range(SUB):
        if group % (SUB // CUTS) == 0:
            part = group // (SUB // CUTS)
            made[2 + 2 * part].wait()
            made[3 + 2 * part].wait()
        lanes = slice(group * LANES, (group + 1) * LANES)
        ext_key[PAD : PAD + rows, :] = key_buf[:, lanes].astype(F32)
        ext_value[PAD : PAD + rows, :] = value_buf[:, lanes].astype(F32)
        gated = short_taps(ext_key, taps_buf, 1, lanes, rows) * short_taps(ext_value, taps_buf, 2, lanes, rows)
        base = group * pitch
        gated_ref[base : base + rows, :] = gated.astype(BF16).astype(F32)
        gated_ref[base : base + 2, :] = jnp.zeros((2, LANES), F32)
        gated_ref[base + rows : base + pitch, :] = jnp.zeros((PAD, LANES), F32)
        for place, (ext, row) in enumerate(
            ((ext_key, 0), (ext_key, 1), (ext_value, 0), (ext_value, 1))
        ):
            at = STATE_ROWS + place * SUB + group
            payload_ref[at : at + 1, :] = ext[PAD + row : PAD + row + 1, :]
        for place, (ext, row) in enumerate(
            ((ext_key, rows - 2), (ext_key, rows - 1), (ext_value, rows - 2), (ext_value, rows - 1))
        ):
            at = STATE_ROWS + (HEADS + 2 + place) * SUB + group
            payload_ref[at : at + 1, :] = ext[PAD + row : PAD + row + 1, :]
    decay = [jnp.exp(-rate_ref[m * SUB : (m + 1) * SUB, :]) for m in range(MODES)]

    def step(t, carry):
        now = gated_ref[pl.ds(t, SUB, stride=pitch), :]
        return tuple(decay[m] * carry[m] + now for m in range(MODES))

    final = lax.fori_loop(0, rows, step, tuple(jnp.zeros((SUB, LANES), F32) for _ in range(MODES)), unroll=8)
    for m in range(MODES):
        payload_ref[m * SUB : (m + 1) * SUB, :] = final[m]
    for one in made[2 + 2 * CUTS :]:
        one.wait()
    to_rows(residue_buf, residue_ref)
    last = query_buf[...].astype(F32)
    for place, row in enumerate((14, 15)):
        for group in range(SUB):
            at = STATE_ROWS + (HEADS + place) * SUB + group
            payload_ref[at : at + 1, :] = last[row : row + 1, group * LANES : (group + 1) * LANES]
    sent_ref[...] = payload_ref[...].astype(BF16)
    for stream in range(3):
        for tap in range(SHORT):
            for group in range(SUB):
                at = (stream * SHORT + tap) * SUB + group
                taps_ref[at : at + 1, :] = taps_buf[stream, tap : tap + 1, group * LANES : (group + 1) * LANES]


def local_kernel(gated_ref, rate_ref, residue_ref, skip_ref, local_ref, conv):
    rows = local_ref.shape[0]
    pitch = rows + PAD
    decay = [jnp.exp(-rate_ref[m * SUB : (m + 1) * SUB, :]) for m in range(MODES)]

    def step(t, carry):
        now = gated_ref[pl.ds(t, SUB, stride=pitch), :]
        fresh = tuple(decay[m] * carry[m] + now for m in range(MODES))
        conv[pl.ds(t, SUB, stride=pitch), :] = summed(
            residue_ref[m * SUB : (m + 1) * SUB, :] * fresh[m] for m in range(MODES)
        )
        return fresh

    lax.fori_loop(0, rows, step, tuple(jnp.zeros((SUB, LANES), F32) for _ in range(MODES)), unroll=8)
    for group in range(SUB):
        lanes = slice(group * LANES, (group + 1) * LANES)
        spot = slice(group * pitch, group * pitch + rows)
        local_ref[:, lanes] = conv[spot, :] + skip_ref[group : group + 1, :] * gated_ref[spot, :]


def query_kernel(query_hbm, taps_ref, query_ref, query_buf, ext, sems):
    rows = query_ref.shape[0]
    made = copies([(query_hbm, query_buf)], sems)
    ext[0:PAD, :] = jnp.zeros((PAD, LANES), F32)
    made[0].wait()
    for group in range(SUB):
        lanes = slice(group * LANES, (group + 1) * LANES)
        ext[PAD : PAD + rows, :] = query_buf[:, lanes].astype(F32)
        tap = [taps_ref[p * SUB + group : p * SUB + group + 1, :] for p in range(SHORT)]
        query_ref[:, lanes] = (
            tap[0] * ext[PAD : PAD + rows, :]
            + tap[1] * ext[PAD - 1 : PAD - 1 + rows, :]
            + tap[2] * ext[PAD - 2 : PAD - 2 + rows, :]
        )


def ahead_kernel(weight_hbm, weight_ref, sems):
    for one in fetch_weight(weight_hbm, weight_ref, sems, weight_hbm.shape[1] - RIGHT_TILES * COLUMN_TILE):
        one.wait()


def project(mixed, weight_buf, fetched, outs):
    piece = mixed.shape[0] // len(outs)
    tiles, _, width = weight_buf.shape
    for i in range(tiles):
        if fetched is not None:
            fetched[i].wait()
        where = slice(i * width, (i + 1) * width)
        product = jnp.dot(mixed[...], weight_buf[i], preferred_element_type=F32)
        for place, out in enumerate(outs):
            out[:, where] = product[place * piece : (place + 1) * piece].astype(out.dtype)


def across_kernel(
    place_ref, local_ref, query_ref, after_ref, fix_ref, rate_ref, residue_ref, weight_ref,
    right_ref, mixed_ref,
    coef,
):
    mix(place_ref, local_ref, query_ref, after_ref, fix_ref, rate_ref, residue_ref, mixed_ref, coef)
    project(mixed_ref, weight_ref, None, [right_ref])


def left_kernel(mixed_ref, weight_hbm, left_two, left_three, weight_buf, sems):
    fetched = fetch_weight(weight_hbm, weight_buf, sems, 0)
    project(mixed_ref, weight_buf, fetched, [left_two, left_three])


def own_kernel(
    place_ref, local_ref, query_ref, after_ref, fix_ref, rate_ref, residue_ref, weight_hbm,
    beside_ref, own_ref,
    mixed, coef, weight_buf, sems,
):
    fetched = fetch_weight(weight_hbm, weight_buf, sems, 0)
    mix(place_ref, local_ref, query_ref, after_ref, fix_ref, rate_ref, residue_ref, mixed, coef)
    project(mixed, weight_buf, fetched, [beside_ref, own_ref])


def mix(place_ref, local_ref, query_ref, after_ref, fix_ref, rate_ref, residue_ref, mixed, coef):
    half_rows = mixed.shape[0]
    piece = half_rows // 2
    base = place_ref[0]
    swap = place_ref[1]
    before = (base - 1).astype(F32)
    coef[...] = residue_ref[...] * after_ref[...] * jnp.exp(-rate_ref[...] * before)
    phase = lax.broadcasted_iota(jnp.int32, (SUB, LANES), 0)
    at_start = base == 0
    row_zero = jnp.logical_and(phase == 0, at_start)
    row_one = jnp.logical_and(phase == 1, at_start)
    zero = jnp.zeros((SUB, LANES), F32)
    for group in range(SUB):
        lanes = slice(group * LANES, (group + 1) * LANES)
        carry, decay = [], []
        for m in range(MODES):
            line = slice(m * SUB + group, m * SUB + group + 1)
            rate = rate_ref[line, :]
            carry.append(jnp.exp(-rate * phase.astype(F32)) * coef[line, :])
            decay.append(jnp.broadcast_to(jnp.exp(-rate * float(SUB)), (SUB, LANES)))

        def fix(i):
            return jnp.broadcast_to(fix_ref[i * SUB + group : i * SUB + group + 1, :], (SUB, LANES))

        for tile in range(0, half_rows, 2 * SUB):
            parts = []
            for inner in range(2):
                offset = tile + inner * SUB
                spot = pl.ds(pl.multiple_of(base + offset, SUB), SUB)
                carried = summed(carry)
                query = query_ref[spot, lanes]
                if offset == 0:
                    carried = jnp.where(row_zero, fix(0), carried) + jnp.where(row_one, fix(1), zero)
                    query = query + jnp.where(row_zero, fix(2), zero) + jnp.where(row_one, fix(3), zero)
                parts.append((local_ref[spot, lanes] + carried) * query)
                carry = [carry[m] * decay[m] for m in range(MODES)]
            block = tile // piece
            row = pl.multiple_of((block ^ swap) * piece + tile % piece, 2 * SUB)
            mixed[pl.ds(row, 2 * SUB), lanes] = jnp.concatenate(parts, axis=0).astype(BF16)


def scan_states(payload, sent, rate, taps, rows, place, count, beside):
    tap = taps.reshape(3, SHORT, SUB, LANES)

    def head_gated(tail, head):
        def filtered(s, first, second, older, newer):
            return (
                tap[s][0] * first + tap[s][1] * newer + tap[s][2] * older,
                tap[s][0] * second + tap[s][1] * first + tap[s][2] * newer,
            )

        keys = filtered(1, head[0], head[1], tail[2], tail[3])
        values = filtered(2, head[2], head[3], tail[4], tail[5])
        return [(k * v).astype(BF16).astype(F32) for k, v in zip(keys, values, strict=True)]

    def decayed(steps):
        return jnp.exp(-rate * steps)

    def joined(pair):
        return decayed(1.0) * pair[0] + pair[1]

    mine = payload.reshape(-1, SUB, LANES)
    own_head = mine[MODES : MODES + HEADS]
    total, head, tail = mine[:MODES], own_head, mine[MODES + HEADS :]
    start = jnp.zeros_like(total)
    border = jnp.zeros_like(tail)
    bits = (count - 1).bit_length()
    for bit in range(bits):
        width = 1 << bit
        mask = width
        if bit >= 2 and bit % 2 == 0 and bit < bits:
            mask = width | (width >> 1)
        sent = beside(bit, sent)
        got = lax.ppermute(sent, "seq", [(j, j ^ mask) for j in range(count)])
        theirs = got.reshape(-1, SUB, LANES).astype(F32)
        upper = ((place >> bit) & 1) == 1
        low = place % width
        length = rows * width
        other_total, other_head, other_tail = theirs[:MODES], theirs[MODES : MODES + HEADS], theirs[MODES + HEADS :]
        low_total = jnp.where(upper, other_total, total)
        low_tail = jnp.where(upper, other_tail, tail)
        high_head = jnp.where(upper, head, other_head)
        entry = joined(head_gated(low_tail, high_head))
        gone = (rows * low).astype(F32)
        start = start + jnp.where(
            upper,
            decayed(gone) * other_total
            + jnp.where(low > 0, decayed(jnp.maximum(gone - 2.0, 0.0)) * entry, 0.0),
            0.0,
        )
        border = jnp.where(jnp.logical_and(upper, low == 0), other_tail, border)
        if bit < bits - 1:
            high_total = jnp.where(upper, total, other_total)
            total = decayed(float(length)) * low_total + high_total + decayed(float(length - 2)) * entry
            tail = jnp.where(upper, tail, other_tail)
        head = jnp.where(upper, other_head, head)
        if bit < bits - 1:
            sent = jnp.concatenate([total, head, tail]).reshape(-1, LANES).astype(BF16)
    first = joined(head_gated(jnp.zeros_like(border), head))
    gone = (rows * place).astype(F32)
    start = start + jnp.where(place > 0, decayed(jnp.maximum(gone - 2.0, 0.0)) * first, 0.0)
    return start, border, head_gated(border, own_head), tap


def on_device(query_stream, key_stream, value_stream, short_filter, decay_rate, residues, skip_bias, out_weight):
    rows, channels = query_stream.shape
    assert channels == SUB * LANES
    columns = out_weight.shape[1]
    pitch = rows + PAD
    count = lax.axis_size("seq")
    place = lax.axis_index("seq")
    parts = lax.axis_size("chan")
    mine = lax.axis_index("chan")
    assert parts == 4
    piece = rows // parts
    query_stream, key_stream, value_stream, short_filter, out_weight, rates, residues, skips = (
        pltpu.with_memory_space_constraint(array, pltpu.HBM)
        for array in (
            query_stream, key_stream, value_stream, short_filter, out_weight,
            decay_rate.T, residues.T, skip_bias.reshape(SUB, LANES),
        )
    )
    params = pltpu.CompilerParams(vmem_limit_bytes=VMEM_LIMIT)
    dma = pltpu.SemaphoreType.DMA
    payload, sent, rate, gated, taps, residue, skip = pl.pallas_call(
        state_kernel,
        out_shape=(
            jax.ShapeDtypeStruct((PAYLOAD, LANES), F32),
            jax.ShapeDtypeStruct((PAYLOAD, LANES), BF16),
            jax.ShapeDtypeStruct((STATE_ROWS, LANES), F32),
            jax.ShapeDtypeStruct((SUB * pitch, LANES), F32),
            jax.ShapeDtypeStruct((3 * SHORT * SUB, LANES), F32),
            jax.ShapeDtypeStruct((STATE_ROWS, LANES), F32),
            jax.ShapeDtypeStruct((SUB, LANES), F32),
        ),
        in_specs=[HBM] * 7,
        out_specs=(VMEM,) * 7,
        scratch_shapes=[
            pltpu.VMEM((rows, channels), BF16),
            pltpu.VMEM((rows, channels), BF16),
            pltpu.VMEM((16, channels), BF16),
            pltpu.VMEM((3, SHORT, channels), F32),
            pltpu.VMEM((MODES, channels), F32),
            pltpu.VMEM((MODES, channels), F32),
            pltpu.VMEM((pitch, LANES), F32),
            pltpu.VMEM((pitch, LANES), F32),
            dma((5 + 2 * CUTS,)),
        ],
        compiler_params=params,
        cost_estimate=pl.CostEstimate(flops=20_000_000, bytes_accessed=3_000_000, transcendentals=0),
    )(query_stream, key_stream, value_stream, short_filter, rates, residues, skips)
    right_side = RIGHT_TILES * COLUMN_TILE
    left_side = columns - right_side
    aside = {}

    light = pl.CostEstimate(flops=1_000_000, bytes_accessed=100_000, transcendentals=0)

    def local_part(gated):
        return pl.pallas_call(
            local_kernel,
            out_shape=jax.ShapeDtypeStruct((rows, channels), F32),
            in_specs=[VMEM] * 4,
            out_specs=VMEM,
            scratch_shapes=[pltpu.VMEM((SUB * pitch, LANES), F32)],
            compiler_params=params,
            cost_estimate=light,
        )(gated, rate, residue, skip)

    def query_part(taps):
        return pl.pallas_call(
            query_kernel,
            out_shape=jax.ShapeDtypeStruct((rows, channels), F32),
            in_specs=[HBM, VMEM],
            out_specs=VMEM,
            scratch_shapes=[
                pltpu.VMEM((rows, channels), BF16),
                pltpu.VMEM((pitch, LANES), F32),
                dma((1,)),
            ],
            compiler_params=params,
            cost_estimate=pl.CostEstimate(flops=1_000_000, bytes_accessed=100_000, transcendentals=0),
        )(query_stream, taps)

    def weight_part(out_weight):
        return pl.pallas_call(
            ahead_kernel,
            out_shape=jax.ShapeDtypeStruct((RIGHT_TILES, channels, COLUMN_TILE), BF16),
            in_specs=[HBM],
            out_specs=VMEM,
            scratch_shapes=[dma((RIGHT_TILES,))],
            compiler_params=params,
            cost_estimate=light,
        )(out_weight)

    def beside_scan(bit, sent):
        last = (count - 1).bit_length() - 1
        if bit == last - 2:
            sent, aside["local"] = lax.optimization_barrier((sent, gated))
        elif bit == last - 1:
            aside["local"] = local_part(aside["local"])
            sent, aside["local"], aside["query"] = lax.optimization_barrier((sent, aside["local"], taps))
        elif bit == last:
            aside["query"] = query_part(aside["query"])
            sent, aside["query"], weight = lax.optimization_barrier((sent, aside["query"], out_weight))
            aside["right"] = weight_part(weight)
        return sent

    rate_rows = rate.reshape(MODES, SUB, LANES)
    start, border, gates, tap = scan_states(payload, sent, rate_rows, taps, rows, place, count, beside_scan)
    local = aside["local"]
    query = aside["query"]
    residue_rows = residue.reshape(MODES, SUB, LANES)
    after_zero = jnp.exp(-rate_rows) * start + gates[0]
    after_one = jnp.exp(-rate_rows) * after_zero + gates[1]
    fixes = jnp.concatenate(
        [
            jnp.sum(residue_rows * after_zero, axis=0) + skip * gates[0],
            skip * gates[1],
            tap[0][1] * border[1] + tap[0][2] * border[0],
            tap[0][2] * border[1],
        ]
    )

    def half_inputs(half, swap):
        at = jnp.stack([half * 2 * piece, swap]).astype(jnp.int32)
        return at, local, query, after_one.reshape(STATE_ROWS, LANES), fixes, rate, residue

    def sent_by(block, pairs):
        return lax.ppermute(block, "chan", pairs)

    def across(step):
        return [(j, j ^ step) for j in range(parts)]

    own_half, odd = mine // 2, mine % 2
    right, mixed = pl.pallas_call(
        across_kernel,
        out_shape=(
            jax.ShapeDtypeStruct((2 * piece, right_side), BF16),
            jax.ShapeDtypeStruct((2 * piece, channels), BF16),
        ),
        in_specs=[SMEM] + [VMEM] * 7,
        out_specs=(VMEM,) * 2,
        scratch_shapes=[pltpu.VMEM((STATE_ROWS, LANES), F32)],
        compiler_params=params,
        cost_estimate=light,
    )(*half_inputs(1 - own_half, odd), aside["right"])
    left_tiles, tiles = left_side // COLUMN_TILE, columns // COLUMN_TILE
    left_two, left_three = pl.pallas_call(
        left_kernel,
        out_shape=(jax.ShapeDtypeStruct((piece, left_side), BF16),) * 2,
        in_specs=[VMEM, HBM],
        out_specs=(VMEM,) * 2,
        scratch_shapes=[pltpu.VMEM((left_tiles, channels, COLUMN_TILE), BF16), dma((left_tiles,))],
        compiler_params=params,
        cost_estimate=light,
    )(mixed, out_weight)
    handed = sent_by(right, [(0, 1), (3, 2)])
    got_two, got_three = sent_by(left_two, across(2)), sent_by(left_three, across(3))
    beside, own = pl.pallas_call(
        own_kernel,
        out_shape=(
            jax.ShapeDtypeStruct((piece, columns), BF16),
            jax.ShapeDtypeStruct((piece, columns), F32),
        ),
        in_specs=[SMEM] + [VMEM] * 6 + [HBM],
        out_specs=(VMEM,) * 2,
        scratch_shapes=[
            pltpu.VMEM((2 * piece, channels), BF16),
            pltpu.VMEM((STATE_ROWS, LANES), F32),
            pltpu.VMEM((tiles, channels, COLUMN_TILE), BF16),
            dma((tiles,)),
        ],
        compiler_params=params,
        cost_estimate=light,
    )(*half_inputs(own_half, 1 - odd), out_weight)
    got_one = sent_by(beside, across(1))
    joined_two = (right[:piece].astype(F32) + handed[piece:].astype(F32)).astype(BF16)
    handed, _ = lax.optimization_barrier((handed, joined_two))
    joined_three = (right[piece:].astype(F32) + handed[:piece].astype(F32)).astype(BF16)
    far_two = sent_by(joined_two, [(1, 3), (2, 0)])
    far_three = sent_by(joined_three, [(1, 2), (2, 1)])
    left = got_two.astype(F32) + got_three.astype(F32)
    far = far_two.astype(F32) + far_three.astype(F32)
    total = own + got_one.astype(F32) + jnp.concatenate([left, far], axis=1)
    return total.astype(BF16)


def solution(mesh):
    return jax.shard_map(
        on_device,
        mesh=mesh,
        in_specs=(
            P("seq", "chan"),
            P("seq", "chan"),
            P("seq", "chan"),
            P(None, None, "chan"),
            P("chan", None),
            P("chan", None),
            P("chan"),
            P("chan", None),
        ),
        out_specs=P(("seq", "chan"), None),
        check_vma=False,
    )
```

```python
import jax
import jax.numpy as jnp
from jax import lax
from jax.experimental import pallas as pl
from jax.experimental.pallas import tpu as pltpu
from jax.sharding import PartitionSpec as P

MODES = 16
SHORT = 3
F32 = jnp.float32
BF16 = jnp.bfloat16
LANES = 128
SUB = 8
PAD = 8
STATE_ROWS = MODES * SUB
HEADS = 4
TAILS = 6
PAYLOAD = STATE_ROWS + SUB * (HEADS + TAILS)
COLUMN_TILE = 512
RIGHT_TILES = 5
CUTS = 4
VMEM_LIMIT = 20 * 1024 * 1024
HBM = pl.BlockSpec(memory_space=pltpu.HBM)
VMEM = pl.BlockSpec(memory_space=pltpu.VMEM)
SMEM = pl.BlockSpec(memory_space=pltpu.SMEM)


def summed(terms):
    terms = list(terms)
    while len(terms) > 1:
        terms = [terms[i] + terms[i + 1] for i in range(0, len(terms), 2)]
    return terms[0]


def short_taps(ext, taps_ref, stream, lanes, count):
    return (
        taps_ref[stream, 0:1, lanes] * ext[PAD : PAD + count, :]
        + taps_ref[stream, 1:2, lanes] * ext[PAD - 1 : PAD - 1 + count, :]
        + taps_ref[stream, 2:3, lanes] * ext[PAD - 2 : PAD - 2 + count, :]
    )


def to_rows(source, target):
    for group in range(SUB):
        target[pl.ds(group, MODES, stride=SUB), :] = source[:, group * LANES : (group + 1) * LANES]


def copies(pairs, sems):
    made = [pltpu.make_async_copy(a, b, sems.at[i]) for i, (a, b) in enumerate(pairs)]
    for one in made:
        one.start()
    return made


def fetch_weight(weight_hbm, weight_buf, sems, first):
    tiles, _, width = weight_buf.shape
    made = [
        pltpu.make_async_copy(weight_hbm.at[:, pl.ds(first + i * width, width)], weight_buf.at[i], sems.at[i])
        for i in range(tiles)
    ]
    for one in made:
        one.start()
    return made


def state_kernel(
    query_hbm, key_hbm, value_hbm, taps_hbm, rate_hbm, residue_hbm, skip_hbm,
    payload_ref, sent_ref, rate_ref, gated_ref, taps_ref, residue_ref, skip_ref,
    key_buf, value_buf, query_buf, taps_buf, rate_buf, residue_buf, ext_key, ext_value, sems,
):
    rows, channels = key_buf.shape
    pitch = rows + PAD
    width = channels // CUTS
    made = copies(
        [(rate_hbm, rate_buf), (taps_hbm, taps_buf)]
        + [
            (hbm.at[:, pl.ds(part * width, width)], buf.at[:, pl.ds(part * width, width)])
            for part in range(CUTS)
            for hbm, buf in ((key_hbm, key_buf), (value_hbm, value_buf))
        ]
        + [(query_hbm.at[pl.ds(rows - 16, 16), :], query_buf), (residue_hbm, residue_buf), (skip_hbm, skip_ref)],
        sems,
    )
    ext_key[0:PAD, :] = jnp.zeros((PAD, LANES), F32)
    ext_value[0:PAD, :] = jnp.zeros((PAD, LANES), F32)
    made[0].wait()
    to_rows(rate_buf, rate_ref)
    made[1].wait()
    for group in range(SUB):
        if group % (SUB // CUTS) == 0:
            part = group // (SUB // CUTS)
            made[2 + 2 * part].wait()
            made[3 + 2 * part].wait()
        lanes = slice(group * LANES, (group + 1) * LANES)
        ext_key[PAD : PAD + rows, :] = key_buf[:, lanes].astype(F32)
        ext_value[PAD : PAD + rows, :] = value_buf[:, lanes].astype(F32)
        gated = short_taps(ext_key, taps_buf, 1, lanes, rows) * short_taps(ext_value, taps_buf, 2, lanes, rows)
        base = group * pitch
        gated_ref[base : base + rows, :] = gated.astype(BF16).astype(F32)
        gated_ref[base : base + 2, :] = jnp.zeros((2, LANES), F32)
        gated_ref[base + rows : base + pitch, :] = jnp.zeros((PAD, LANES), F32)
        for place, (ext, row) in enumerate(
            ((ext_key, 0), (ext_key, 1), (ext_value, 0), (ext_value, 1))
        ):
            at = STATE_ROWS + place * SUB + group
            payload_ref[at : at + 1, :] = ext[PAD + row : PAD + row + 1, :]
        for place, (ext, row) in enumerate(
            ((ext_key, rows - 2), (ext_key, rows - 1), (ext_value, rows - 2), (ext_value, rows - 1))
        ):
            at = STATE_ROWS + (HEADS + 2 + place) * SUB + group
            payload_ref[at : at + 1, :] = ext[PAD + row : PAD + row + 1, :]
    decay = [jnp.exp(-rate_ref[m * SUB : (m + 1) * SUB, :]) for m in range(MODES)]

    def step(t, carry):
        now = gated_ref[pl.ds(t, SUB, stride=pitch), :]
        return tuple(decay[m] * carry[m] + now for m in range(MODES))

    final = lax.fori_loop(0, rows, step, tuple(jnp.zeros((SUB, LANES), F32) for _ in range(MODES)), unroll=8)
    for m in range(MODES):
        payload_ref[m * SUB : (m + 1) * SUB, :] = final[m]
    for one in made[2 + 2 * CUTS :]:
        one.wait()
    to_rows(residue_buf, residue_ref)
    last = query_buf[...].astype(F32)
    for place, row in enumerate((14, 15)):
        for group in range(SUB):
            at = STATE_ROWS + (HEADS + place) * SUB + group
            payload_ref[at : at + 1, :] = last[row : row + 1, group * LANES : (group + 1) * LANES]
    sent_ref[...] = payload_ref[...].astype(BF16)
    for stream in range(3):
        for tap in range(SHORT):
            for group in range(SUB):
                at = (stream * SHORT + tap) * SUB + group
                taps_ref[at : at + 1, :] = taps_buf[stream, tap : tap + 1, group * LANES : (group + 1) * LANES]


def local_kernel(gated_ref, rate_ref, residue_ref, skip_ref, local_ref, conv):
    rows = local_ref.shape[0]
    pitch = rows + PAD
    decay = [jnp.exp(-rate_ref[m * SUB : (m + 1) * SUB, :]) for m in range(MODES)]

    def step(t, carry):
        now = gated_ref[pl.ds(t, SUB, stride=pitch), :]
        fresh = tuple(decay[m] * carry[m] + now for m in range(MODES))
        conv[pl.ds(t, SUB, stride=pitch), :] = summed(
            residue_ref[m * SUB : (m + 1) * SUB, :] * fresh[m] for m in range(MODES)
        )
        return fresh

    lax.fori_loop(0, rows, step, tuple(jnp.zeros((SUB, LANES), F32) for _ in range(MODES)), unroll=8)
    for group in range(SUB):
        lanes = slice(group * LANES, (group + 1) * LANES)
        spot = slice(group * pitch, group * pitch + rows)
        local_ref[:, lanes] = conv[spot, :] + skip_ref[group : group + 1, :] * gated_ref[spot, :]


def query_kernel(query_hbm, taps_ref, query_ref, query_buf, ext, sems):
    rows = query_ref.shape[0]
    made = copies([(query_hbm, query_buf)], sems)
    ext[0:PAD, :] = jnp.zeros((PAD, LANES), F32)
    made[0].wait()
    for group in range(SUB):
        lanes = slice(group * LANES, (group + 1) * LANES)
        ext[PAD : PAD + rows, :] = query_buf[:, lanes].astype(F32)
        tap = [taps_ref[p * SUB + group : p * SUB + group + 1, :] for p in range(SHORT)]
        query_ref[:, lanes] = (
            tap[0] * ext[PAD : PAD + rows, :]
            + tap[1] * ext[PAD - 1 : PAD - 1 + rows, :]
            + tap[2] * ext[PAD - 2 : PAD - 2 + rows, :]
        )


def ahead_kernel(weight_hbm, weight_ref, sems):
    for one in fetch_weight(weight_hbm, weight_ref, sems, weight_hbm.shape[1] - RIGHT_TILES * COLUMN_TILE):
        one.wait()


def project(mixed, weight_buf, fetched, outs):
    piece = mixed.shape[0] // len(outs)
    tiles, _, width = weight_buf.shape
    for i in range(tiles):
        if fetched is not None:
            fetched[i].wait()
        where = slice(i * width, (i + 1) * width)
        product = jnp.dot(mixed[...], weight_buf[i], preferred_element_type=F32)
        for place, out in enumerate(outs):
            out[:, where] = product[place * piece : (place + 1) * piece].astype(out.dtype)


def across_kernel(
    place_ref, local_ref, query_ref, after_ref, fix_ref, rate_ref, residue_ref, weight_ref,
    right_ref, mixed_ref,
    coef,
):
    mix(place_ref, local_ref, query_ref, after_ref, fix_ref, rate_ref, residue_ref, mixed_ref, coef)
    project(mixed_ref, weight_ref, None, [right_ref])


def left_kernel(mixed_ref, weight_hbm, left_two, left_three, weight_buf, sems):
    fetched = fetch_weight(weight_hbm, weight_buf, sems, 0)
    project(mixed_ref, weight_buf, fetched, [left_two, left_three])


def own_kernel(
    place_ref, local_ref, query_ref, after_ref, fix_ref, rate_ref, residue_ref, weight_hbm,
    beside_ref, own_ref,
    mixed, coef, weight_buf, sems,
):
    fetched = fetch_weight(weight_hbm, weight_buf, sems, 0)
    mix(place_ref, local_ref, query_ref, after_ref, fix_ref, rate_ref, residue_ref, mixed, coef)
    project(mixed, weight_buf, fetched, [beside_ref, own_ref])


def mix(place_ref, local_ref, query_ref, after_ref, fix_ref, rate_ref, residue_ref, mixed, coef):
    half_rows = mixed.shape[0]
    piece = half_rows // 2
    base = place_ref[0]
    swap = place_ref[1]
    before = (base - 1).astype(F32)
    coef[0:STATE_ROWS, :] = residue_ref[...] * after_ref[...] * jnp.exp(-rate_ref[...] * before)
    for k in range(4):
        coef[(k + 1) * STATE_ROWS : (k + 2) * STATE_ROWS, :] = jnp.exp(-rate_ref[...] * float(1 << k))
    phase = lax.broadcasted_iota(jnp.int32, (SUB, LANES), 0)
    bits = [((phase >> k) & 1) == 1 for k in range(3)]
    at_start = base == 0
    row_zero = jnp.logical_and(phase == 0, at_start)
    row_one = jnp.logical_and(phase == 1, at_start)
    zero = jnp.zeros((SUB, LANES), F32)
    for group in range(SUB):
        lanes = slice(group * LANES, (group + 1) * LANES)
        carry, decay = [], []
        for m in range(MODES):
            line = slice(m * SUB + group, m * SUB + group + 1)
            head = jnp.broadcast_to(coef[line, :], (SUB, LANES))
            for k in range(3):
                row = (k + 1) * STATE_ROWS + m * SUB + group
                head = jnp.where(bits[k], head * coef[row : row + 1, :], head)
            carry.append(head)
            row = 4 * STATE_ROWS + m * SUB + group
            decay.append(jnp.broadcast_to(coef[row : row + 1, :], (SUB, LANES)))

        def fix(i):
            return jnp.broadcast_to(fix_ref[i * SUB + group : i * SUB + group + 1, :], (SUB, LANES))

        for tile in range(0, half_rows, 2 * SUB):
            parts = []
            for inner in range(2):
                offset = tile + inner * SUB
                spot = pl.ds(pl.multiple_of(base + offset, SUB), SUB)
                carried = summed(carry)
                query = query_ref[spot, lanes]
                if offset == 0:
                    carried = jnp.where(row_zero, fix(0), carried) + jnp.where(row_one, fix(1), zero)
                    query = query + jnp.where(row_zero, fix(2), zero) + jnp.where(row_one, fix(3), zero)
                parts.append((local_ref[spot, lanes] + carried) * query)
                carry = [carry[m] * decay[m] for m in range(MODES)]
            block = tile // piece
            row = pl.multiple_of((block ^ swap) * piece + tile % piece, 2 * SUB)
            mixed[pl.ds(row, 2 * SUB), lanes] = jnp.concatenate(parts, axis=0).astype(BF16)


def scan_states(payload, sent, rate, taps, rows, place, count, beside):
    tap = taps.reshape(3, SHORT, SUB, LANES)

    def head_gated(tail, head):
        def filtered(s, first, second, older, newer):
            return (
                tap[s][0] * first + tap[s][1] * newer + tap[s][2] * older,
                tap[s][0] * second + tap[s][1] * first + tap[s][2] * newer,
            )

        keys = filtered(1, head[0], head[1], tail[2], tail[3])
        values = filtered(2, head[2], head[3], tail[4], tail[5])
        return [(k * v).astype(BF16).astype(F32) for k, v in zip(keys, values, strict=True)]

    def decayed(steps):
        return jnp.exp(-rate * steps)

    def joined(pair):
        return decayed(1.0) * pair[0] + pair[1]

    mine = payload.reshape(-1, SUB, LANES)
    own_head = mine[MODES : MODES + HEADS]
    total, head, tail = mine[:MODES], own_head, mine[MODES + HEADS :]
    start = jnp.zeros_like(total)
    border = jnp.zeros_like(tail)
    bits = (count - 1).bit_length()
    for bit in range(bits):
        width = 1 << bit
        mask = width
        if bit >= 2 and bit % 2 == 0 and bit < bits:
            mask = width | (width >> 1)
        sent = beside(bit, sent)
        got = lax.ppermute(sent, "seq", [(j, j ^ mask) for j in range(count)])
        theirs = got.reshape(-1, SUB, LANES).astype(F32)
        upper = ((place >> bit) & 1) == 1
        low = place % width
        length = rows * width
        other_total, other_head, other_tail = theirs[:MODES], theirs[MODES : MODES + HEADS], theirs[MODES + HEADS :]
        low_total = jnp.where(upper, other_total, total)
        low_tail = jnp.where(upper, other_tail, tail)
        high_head = jnp.where(upper, head, other_head)
        entry = joined(head_gated(low_tail, high_head))
        gone = (rows * low).astype(F32)
        start = start + jnp.where(
            upper,
            decayed(gone) * other_total
            + jnp.where(low > 0, decayed(jnp.maximum(gone - 2.0, 0.0)) * entry, 0.0),
            0.0,
        )
        border = jnp.where(jnp.logical_and(upper, low == 0), other_tail, border)
        if bit < bits - 1:
            high_total = jnp.where(upper, total, other_total)
            total = decayed(float(length)) * low_total + high_total + decayed(float(length - 2)) * entry
            tail = jnp.where(upper, tail, other_tail)
        head = jnp.where(upper, other_head, head)
        if bit < bits - 1:
            sent = jnp.concatenate([total, head, tail]).reshape(-1, LANES).astype(BF16)
    first = joined(head_gated(jnp.zeros_like(border), head))
    gone = (rows * place).astype(F32)
    start = start + jnp.where(place > 0, decayed(jnp.maximum(gone - 2.0, 0.0)) * first, 0.0)
    return start, border, head_gated(border, own_head), tap


def on_device(query_stream, key_stream, value_stream, short_filter, decay_rate, residues, skip_bias, out_weight):
    rows, channels = query_stream.shape
    assert channels == SUB * LANES
    columns = out_weight.shape[1]
    pitch = rows + PAD
    count = lax.axis_size("seq")
    place = lax.axis_index("seq")
    parts = lax.axis_size("chan")
    mine = lax.axis_index("chan")
    assert parts == 4
    piece = rows // parts
    query_stream, key_stream, value_stream, short_filter, out_weight, rates, residues, skips = (
        pltpu.with_memory_space_constraint(array, pltpu.HBM)
        for array in (
            query_stream, key_stream, value_stream, short_filter, out_weight,
            decay_rate.T, residues.T, skip_bias.reshape(SUB, LANES),
        )
    )
    params = pltpu.CompilerParams(vmem_limit_bytes=VMEM_LIMIT)
    dma = pltpu.SemaphoreType.DMA
    payload, sent, rate, gated, taps, residue, skip = pl.pallas_call(
        state_kernel,
        out_shape=(
            jax.ShapeDtypeStruct((PAYLOAD, LANES), F32),
            jax.ShapeDtypeStruct((PAYLOAD, LANES), BF16),
            jax.ShapeDtypeStruct((STATE_ROWS, LANES), F32),
            jax.ShapeDtypeStruct((SUB * pitch, LANES), F32),
            jax.ShapeDtypeStruct((3 * SHORT * SUB, LANES), F32),
            jax.ShapeDtypeStruct((STATE_ROWS, LANES), F32),
            jax.ShapeDtypeStruct((SUB, LANES), F32),
        ),
        in_specs=[HBM] * 7,
        out_specs=(VMEM,) * 7,
        scratch_shapes=[
            pltpu.VMEM((rows, channels), BF16),
            pltpu.VMEM((rows, channels), BF16),
            pltpu.VMEM((16, channels), BF16),
            pltpu.VMEM((3, SHORT, channels), F32),
            pltpu.VMEM((MODES, channels), F32),
            pltpu.VMEM((MODES, channels), F32),
            pltpu.VMEM((pitch, LANES), F32),
            pltpu.VMEM((pitch, LANES), F32),
            dma((5 + 2 * CUTS,)),
        ],
        compiler_params=params,
        cost_estimate=pl.CostEstimate(flops=20_000_000, bytes_accessed=3_000_000, transcendentals=0),
    )(query_stream, key_stream, value_stream, short_filter, rates, residues, skips)
    right_side = RIGHT_TILES * COLUMN_TILE
    left_side = columns - right_side
    aside = {}

    light = pl.CostEstimate(flops=1_000_000, bytes_accessed=100_000, transcendentals=0)

    def local_part(gated):
        return pl.pallas_call(
            local_kernel,
            out_shape=jax.ShapeDtypeStruct((rows, channels), F32),
            in_specs=[VMEM] * 4,
            out_specs=VMEM,
            scratch_shapes=[pltpu.VMEM((SUB * pitch, LANES), F32)],
            compiler_params=params,
            cost_estimate=light,
        )(gated, rate, residue, skip)

    def query_part(taps):
        return pl.pallas_call(
            query_kernel,
            out_shape=jax.ShapeDtypeStruct((rows, channels), F32),
            in_specs=[HBM, VMEM],
            out_specs=VMEM,
            scratch_shapes=[
                pltpu.VMEM((rows, channels), BF16),
                pltpu.VMEM((pitch, LANES), F32),
                dma((1,)),
            ],
            compiler_params=params,
            cost_estimate=pl.CostEstimate(flops=1_000_000, bytes_accessed=100_000, transcendentals=0),
        )(query_stream, taps)

    def weight_part(out_weight):
        return pl.pallas_call(
            ahead_kernel,
            out_shape=jax.ShapeDtypeStruct((RIGHT_TILES, channels, COLUMN_TILE), BF16),
            in_specs=[HBM],
            out_specs=VMEM,
            scratch_shapes=[dma((RIGHT_TILES,))],
            compiler_params=params,
            cost_estimate=light,
        )(out_weight)

    def beside_scan(bit, sent):
        last = (count - 1).bit_length() - 1
        if bit == last - 2:
            sent, aside["local"] = lax.optimization_barrier((sent, gated))
        elif bit == last - 1:
            aside["local"] = local_part(aside["local"])
            sent, aside["local"], aside["query"] = lax.optimization_barrier((sent, aside["local"], taps))
        elif bit == last:
            aside["query"] = query_part(aside["query"])
            sent, aside["query"], weight = lax.optimization_barrier((sent, aside["query"], out_weight))
            aside["right"] = weight_part(weight)
        return sent

    rate_rows = rate.reshape(MODES, SUB, LANES)
    start, border, gates, tap = scan_states(payload, sent, rate_rows, taps, rows, place, count, beside_scan)
    local = aside["local"]
    query = aside["query"]
    residue_rows = residue.reshape(MODES, SUB, LANES)
    after_zero = jnp.exp(-rate_rows) * start + gates[0]
    after_one = jnp.exp(-rate_rows) * after_zero + gates[1]
    fixes = jnp.concatenate(
        [
            jnp.sum(residue_rows * after_zero, axis=0) + skip * gates[0],
            skip * gates[1],
            tap[0][1] * border[1] + tap[0][2] * border[0],
            tap[0][2] * border[1],
        ]
    )

    def half_inputs(half, swap):
        at = jnp.stack([half * 2 * piece, swap]).astype(jnp.int32)
        return at, local, query, after_one.reshape(STATE_ROWS, LANES), fixes, rate, residue

    def sent_by(block, pairs):
        return lax.ppermute(block, "chan", pairs)

    def across(step):
        return [(j, j ^ step) for j in range(parts)]

    own_half, odd = mine // 2, mine % 2
    right, mixed = pl.pallas_call(
        across_kernel,
        out_shape=(
            jax.ShapeDtypeStruct((2 * piece, right_side), BF16),
            jax.ShapeDtypeStruct((2 * piece, channels), BF16),
        ),
        in_specs=[SMEM] + [VMEM] * 7,
        out_specs=(VMEM,) * 2,
        scratch_shapes=[pltpu.VMEM((5 * STATE_ROWS, LANES), F32)],
        compiler_params=params,
        cost_estimate=light,
    )(*half_inputs(1 - own_half, odd), aside["right"])
    left_tiles, tiles = left_side // COLUMN_TILE, columns // COLUMN_TILE
    left_two, left_three = pl.pallas_call(
        left_kernel,
        out_shape=(jax.ShapeDtypeStruct((piece, left_side), BF16),) * 2,
        in_specs=[VMEM, HBM],
        out_specs=(VMEM,) * 2,
        scratch_shapes=[pltpu.VMEM((left_tiles, channels, COLUMN_TILE), BF16), dma((left_tiles,))],
        compiler_params=params,
        cost_estimate=light,
    )(mixed, out_weight)
    handed = sent_by(right, [(0, 1), (3, 2)])
    got_two, got_three = sent_by(left_two, across(2)), sent_by(left_three, across(3))
    beside, own = pl.pallas_call(
        own_kernel,
        out_shape=(
            jax.ShapeDtypeStruct((piece, columns), BF16),
            jax.ShapeDtypeStruct((piece, columns), F32),
        ),
        in_specs=[SMEM] + [VMEM] * 6 + [HBM],
        out_specs=(VMEM,) * 2,
        scratch_shapes=[
            pltpu.VMEM((2 * piece, channels), BF16),
            pltpu.VMEM((5 * STATE_ROWS, LANES), F32),
            pltpu.VMEM((tiles, channels, COLUMN_TILE), BF16),
            dma((tiles,)),
        ],
        compiler_params=params,
        cost_estimate=light,
    )(*half_inputs(own_half, 1 - odd), out_weight)
    got_one = sent_by(beside, across(1))
    joined_two = (right[:piece].astype(F32) + handed[piece:].astype(F32)).astype(BF16)
    handed, _ = lax.optimization_barrier((handed, joined_two))
    joined_three = (right[piece:].astype(F32) + handed[:piece].astype(F32)).astype(BF16)
    far_two = sent_by(joined_two, [(1, 3), (2, 0)])
    far_three = sent_by(joined_three, [(1, 2), (2, 1)])
    left = got_two.astype(F32) + got_three.astype(F32)
    far = far_two.astype(F32) + far_three.astype(F32)
    total = own + got_one.astype(F32) + jnp.concatenate([left, far], axis=1)
    return total.astype(BF16)


def solution(mesh):
    return jax.shard_map(
        on_device,
        mesh=mesh,
        in_specs=(
            P("seq", "chan"),
            P("seq", "chan"),
            P("seq", "chan"),
            P(None, None, "chan"),
            P("chan", None),
            P("chan", None),
            P("chan"),
            P("chan", None),
        ),
        out_specs=P(("seq", "chan"), None),
        check_vma=False,
    )
```
